32 devices in a mesh: line: 4 (over y, core), cross: 8 (over z, x).
Axes of the slice: x: 2, y: 2, z: 4, core: 2. Of those that a mesh axis runs over, the one named last changes fastest.
Arguments:
- jacobian: float32 [5, 5, 128, 1024], P(None, None, 'line', 'cross'), may hold values from -41 to 121, as said below
- time_step: float32 [128, 1024], P('line', 'cross'), may hold values from 2 to 8
- source: bfloat16 [5, 128, 1024], P(None, 'line', 'cross'), may hold values from -12 to 15
- cross_flux: bfloat16 [5, 128, 1024], P(None, 'line', 'cross'), may hold values from -12 to 12
Outputs:
- update: float32 [5, 128, 1024], P(None, 'line', 'cross')
The draws below stay inside these ranges and needn't reach their ends.
Inputs may be any that keep to these rules, and one draw needn't show every extreme that they name: Every 5 x 5 block of jacobian is symmetric, and for every line the system matrix of the last step has a positive definite symmetric part.
All inputs are finite; a program needn't handle non-finite values.
Results may differ from the reference program's by a relative error of at most 0.0003.
Values may be sent and summed in bfloat16 or wider, within the bound.
A program may use at most 64 MiB of HBM per device.

```python
import math
import jax
import jax.numpy as jnp
from jax import lax

NZ = 8
NX = 128
LINES = 1024


drift_period = 512.0


drift_height = 4.0


def draw_jacobian(key, part):
    key_scale, key_mean, key_cell, key_phase, key_drift = jax.random.split(key, 5)
    line_scale = jnp.exp(jax.random.uniform(key_scale, (LINES,), jnp.float32, math.log(8.0), math.log(32.0)))
    base_matrix = jax.random.uniform(key_mean, (5, 5, LINES), jnp.float32, -1.0, 1.0)
    unit_matrix = jnp.eye(5, dtype=jnp.float32)[:, :, None]
    mean_part = line_scale * (2.0 * unit_matrix + 0.5 * (base_matrix + jnp.swapaxes(base_matrix, 0, 1)))
    drift_raw = jax.random.uniform(key_drift, (5, 5, LINES), jnp.float32, -1.0, 1.0)
    drift_matrix = 0.5 * unit_matrix + 0.05 * (drift_raw + jnp.swapaxes(drift_raw, 0, 1))
    phase = jax.random.uniform(key_phase, (LINES,), jnp.float32, 0.0, 2.0 * math.pi)
    position = jnp.arange(NX).astype(jnp.float32)[:, None]
    profile = drift_height * jnp.sin(2.0 * math.pi * position / drift_period + phase[None, :])
    cell_part = jax.random.uniform(key_cell, (5, 5, NX, LINES), jnp.float32, -1.0, 1.0)
    cell_part = 0.005 * (cell_part + jnp.swapaxes(cell_part, 0, 1))
    return mean_part[:, :, None, :] + profile[None, None, :, :] * drift_matrix[:, :, None, :] + cell_part


def draw_source(key, part):
    rough_part = jnp.clip(jax.random.normal(key, (5, NX, LINES), jnp.float32), -4.0, 4.0)
    values = 3.0 * rough_part
    return values.astype(jnp.bfloat16)


def levels(key, extent, cuts, least, top_value):
    def one(axis_at, parts):
        heights = jax.random.uniform(jax.random.fold_in(jax.random.fold_in(key, 6), axis_at), (parts,), jnp.float32, least / len(cuts), top_value / len(cuts))
        return jnp.repeat(jnp.exp(heights), extent[axis_at] // parts).reshape((-1,) + (1,) * (len(extent) - axis_at - 1))

    factor_of = one(*cuts[0])
    for cut in cuts[1:]:
        factor_of = factor_of * one(*cut)
    return factor_of


def gaussian(own_key, dims, width, most, shards=(), kind=jnp.bfloat16):
    values = width * jax.random.normal(own_key, dims, jnp.float32)
    if shards:
        values = values * levels(own_key, dims, shards, -0.22, 0.18)
    return jnp.clip(values, -most, most).astype(kind)


def setup_inputs(seed: int = 0) -> dict:
    splits = jax.random.split(jax.random.key(seed), 5)
    return {
        "jacobian": draw_jacobian(jax.random.fold_in(splits[4], 71), 0),
        "time_step": jnp.clip(jnp.exp(math.log(8.0) - 1.3862944 * jax.random.uniform(splits[1], (NX, LINES), jnp.float32) ** levels(splits[1], (NX, LINES), ((0, 4), (1, 8)), -0.2, 0.2)), 2.0, 8.0),
        "source": draw_source(jax.random.fold_in(splits[4], 71), 0),
        "cross_flux": gaussian(splits[3], (5, NX, LINES), 3.0, 12.0, ((1, 4), (2, 8))),
    }


damping = 0.05


def product(matrix, operand):
    summed = matrix[:, 0][:, None] * operand[0][None]
    for column_index in range(1, matrix.shape[1]):
        summed = summed + matrix[:, column_index][:, None] * operand[column_index][None]
    return summed


def times_vector(matrix, vector):
    return product(matrix, vector[:, None])[:, 0]


def eliminate(matrix, columns):
    unknowns = matrix.shape[0]
    current = jnp.concatenate([matrix, columns], axis=1)
    for column_index in range(unknowns):
        chosen_row = current[column_index]
        pivot_row = chosen_row / chosen_row[column_index][None]
        column_values = current[:, column_index]
        current = current - column_values[:, None] * pivot_row[None]
        current = jnp.concatenate([current[:column_index], pivot_row[None], current[column_index + 1:]], axis=0)
    return current[:, unknowns:]


def reference(jacobian, time_step, source, cross_flux):
    flux_values = cross_flux.astype(jnp.float32)
    padded = jnp.pad(flux_values, ((0, 0), (0, 0), (NZ, NZ)))
    residual = source.astype(jnp.float32) - 0.5 * (padded[:, :, 2 * NZ:] - padded[:, :, :LINES])
    block_width = math.gcd(LINES, 512)
    blocks = LINES // block_width
    unit_matrix = jnp.eye(5, dtype=jnp.float32)[:, :, None]
    inside = jnp.arange(NX)
    has_lower = (inside > 0).astype(jnp.float32)[:, None, None, None]
    has_upper = (inside < NX - 1).astype(jnp.float32)[:, None, None, None]

    def solve_block(number):
        offset = (number * block_width).astype(jnp.int32)
        jac_block = lax.dynamic_slice_in_dim(jacobian, offset, block_width, 3)
        step_part = lax.dynamic_slice_in_dim(time_step, offset, block_width, 1)
        rhs_part = lax.dynamic_slice_in_dim(residual, offset, block_width, 2)
        jac_seq = jnp.moveaxis(jac_block, 2, 0)
        previous = jnp.concatenate([jnp.zeros_like(jac_seq[:1]), jac_seq[:-1]], axis=0)
        following = jnp.concatenate([jac_seq[1:], jnp.zeros_like(jac_seq[:1])], axis=0)
        lower_seq = has_lower * (-previous * 0.5 - damping * unit_matrix)
        upper_seq = has_upper * (following * 0.5 - damping * unit_matrix)
        diagonal_seq = 1.0 / step_part + 2.0 * damping
        rhs_seq = jnp.moveaxis(rhs_part, 1, 0)

        def forward(running, items):
            coupling, reduced = running
            lower_block, upper_block, diagonal, right_side = items
            pivot_block = diagonal * unit_matrix - product(lower_block, coupling)
            source_term = right_side - times_vector(lower_block, reduced)
            solved = eliminate(pivot_block, jnp.concatenate([upper_block, source_term[:, None]], axis=1))
            result = (solved[:, :5], solved[:, 5])
            return result, result

        initial = (jnp.zeros((5, 5, block_width), jnp.float32), jnp.zeros((5, block_width), jnp.float32))
        couplings, reduced_all = lax.scan(forward, initial, (lower_seq, upper_seq, diagonal_seq, rhs_seq))[1]

        def backward(following_value, items):
            coupling, reduced = items
            value = reduced - times_vector(coupling, following_value)
            return value, value

        values = lax.scan(backward, jnp.zeros((5, block_width), jnp.float32), (couplings, reduced_all), reverse=True)[1]
        return jnp.moveaxis(values, 0, 1)

    solved_blocks = lax.map(solve_block, jnp.arange(blocks, dtype=jnp.int32))
    return jnp.moveaxis(solved_blocks, 0, 2).reshape(5, NX, LINES)
```

```python
import functools

import jax
import jax.numpy as jnp
from jax import lax
from jax.experimental import pallas as pl
from jax.experimental.pallas import tpu as pltpu
from jax.sharding import PartitionSpec as P

NZ = 8
UNK = 5
SUB = 8
STEPS = 4
damping = 0.05
MESH = pl.DeviceIdType.MESH


def mm(matrix, operand):
    summed = matrix[:, 0][:, None] * operand[0][None]
    for k in range(1, UNK):
        summed = summed + matrix[:, k][:, None] * operand[k][None]
    return summed


def mv(matrix, vector):
    summed = matrix[:, 0] * vector[0][None]
    for k in range(1, UNK):
        summed = summed + matrix[:, k] * vector[k][None]
    return summed


def inverse(matrix):
    rows = [matrix[i] for i in range(UNK)]
    for k in range(UNK):
        pivot = rows[k]
        scale = 1.0 / pivot[k : k + 1]
        one = jnp.ones_like(scale)
        parts = [pivot[:k]] * (k > 0) + [one] + [pivot[k + 1 :]] * (k < UNK - 1)
        pivot = jnp.concatenate(parts, axis=0) * scale
        rows[k] = pivot
        for i in range(UNK):
            if i == k:
                continue
            row = rows[i]
            factor = row[k : k + 1]
            parts = [row[:k]] * (k > 0) + [jnp.zeros_like(one)] + [row[k + 1 :]] * (k < UNK - 1)
            rows[i] = jnp.concatenate(parts, axis=0) - factor * pivot
    return jnp.stack(rows, axis=0)


def solve_one(matrix, vector):
    rows = [
        jnp.concatenate([matrix[i], vector[i : i + 1]], axis=0) for i in range(UNK)
    ]
    for k in range(UNK):
        pivot = rows[k][1:] * (1.0 / rows[k][:1])
        rows[k] = pivot
        for i in range(UNK):
            if i != k:
                rows[i] = rows[i][1:] - rows[i][:1] * pivot
    return jnp.concatenate(rows, axis=0)


def diagonal_block(values):
    nothing = jnp.zeros_like(values)
    return jnp.stack(
        [jnp.stack([values if i == j else nothing for j in range(UNK)]) for i in range(UNK)]
    )


def kernel(
    line_size, cross_size,
    jac_hbm, step_hbm, source_hbm, flux_hbm, out_ref,
    jac, step, source, flux, res,
    halo_out, halo_in, mats, rhss, last,
    local_sem, halo_send, halo_recv,
    mat_send, mat_recv, rhs_send, rhs_recv, last_send, last_recv,
):
    rounds = line_size.bit_length() - 1
    me = lax.axis_index("line")
    row = lax.axis_index("cross")
    above, below = lax.rem(row + 1, cross_size), lax.rem(row + cross_size - 1, cross_size)
    bits = [lax.rem(me // (1 << r), 2) for r in range(rounds)]
    partners = [me + (1 - 2 * bits[r]) * (1 << r) for r in range(rounds)]

    barrier = pltpu.get_barrier_semaphore()
    targets = [(me, above), (me, below)] + [(partners[r], row) for r in range(rounds)]
    for target in targets:
        pl.semaphore_signal(barrier, inc=1, device_id=target, device_id_type=MESH)

    loads = [
        pltpu.make_async_copy(src, dst, local_sem.at[i])
        for i, (src, dst) in enumerate(
            [(flux_hbm, flux), (jac_hbm, jac), (step_hbm, step), (source_hbm, source)]
        )
    ]
    for load in loads:
        load.start()

    cells = jac.shape[2]
    lines = jac.shape[3]
    loads[0].wait()
    lane = lax.broadcasted_iota(jnp.int32, (cells, lines), 1)
    tails = jnp.zeros((cells, lines), jnp.float32)
    heads = jnp.zeros((cells, lines), jnp.float32)
    for f in range(UNK):
        field = flux[f].astype(jnp.float32)
        inside = (lane >= NZ * f) & (lane < NZ * (f + 1))
        tails = jnp.where(inside, pltpu.roll(field, NZ * (f + 1), 1), tails)
        heads = jnp.where(inside, field if f == 0 else pltpu.roll(field, NZ * f, 1), heads)
    halo_out[0] = tails.astype(jnp.bfloat16)
    halo_out[1] = heads.astype(jnp.bfloat16)

    def remote(src, dst, send, recv, target):
        return pltpu.make_async_remote_copy(
            src_ref=src, dst_ref=dst, send_sem=send, recv_sem=recv,
            device_id=target, device_id_type=MESH,
        )

    for load in loads[1:]:
        load.wait()
    pl.semaphore_wait(barrier, len(targets))
    halo_copies = [
        remote(halo_out.at[0], halo_in.at[0], halo_send.at[0], halo_recv.at[0], (me, above)),
        remote(halo_out.at[1], halo_in.at[1], halo_send.at[1], halo_recv.at[1], (me, below)),
    ]
    for copy in halo_copies:
        copy.start()

    sub = lax.broadcasted_iota(jnp.int32, (SUB, lines), 0)
    unit = diagonal_block(jnp.ones((SUB, lines), jnp.float32))
    diag = []
    for t in range(STEPS):
        diag.append(1.0 / step[pl.ds(t, SUB, stride=STEPS), :] + 2.0 * damping)

    def jac_at(t):
        return jac[:, :, pl.ds(t, SUB, stride=STEPS), :]

    def sub_roll(values, shift):
        shift = shift % SUB
        return values if shift == 0 else pltpu.roll(values, shift, values.ndim - 2)

    def upper(block):
        return block * 0.5 - damping * unit

    def lower(block):
        return block * -0.5 - damping * unit

    over1, over2 = 1.0 / diag[1], 1.0 / diag[2]
    up12, low21 = upper(jac_at(2)), lower(jac_at(1))
    up0, low3 = upper(jac_at(1)), lower(jac_at(2))
    schur1 = inverse(diagonal_block(diag[1]) - mm(up12, low21 * over2))
    schur2 = inverse(diagonal_block(diag[2]) - mm(low21, up12 * over1))
    own1 = mm(schur1, lower(jac_at(0)))
    own2 = mm(schur2, upper(jac_at(3)))
    other1 = -mm(up12, own2) * over1
    other2 = -mm(low21, own1) * over2
    head_diag = diagonal_block(diag[0]) - mm(up0, own1)
    head_link = -mm(up0, other1)
    tail_diag = diagonal_block(diag[3]) - mm(low3, own2)
    tail_link = -mm(low3, other2)

    even = lax.rem(sub, 2) == 0
    inner_diag = jnp.where(even, tail_diag, head_diag)
    inner_link = jnp.where(even, tail_link, head_link)
    outer_diag = jnp.where(even, head_diag, tail_diag)
    outer_link = jnp.where(even, head_link, tail_link)
    to_next = upper(sub_roll(jac_at(0), -1))
    to_last = lower(sub_roll(jac_at(3), 1))
    levels = []
    half = 1
    while half < SUB:
        left = lax.rem(sub, 2 * half) < half

        def swap(x, left=left):
            return jnp.where(left, sub_roll(x, -1), sub_roll(x, 1))

        def out(x, left=left, half=half):
            return x if half == 1 else jnp.where(
                left, sub_roll(x, 1 - half), sub_roll(x, half - 1)
            )

        couple = jnp.where(left, to_next, to_last)
        inv = inverse(inner_diag)
        through = mm(inv, couple)
        schur = inverse(inner_diag - mm(couple, swap(through)))
        own = mm(schur, inner_link)
        other = -mm(through, swap(own))
        levels.append((half, left, swap, out, inv, couple, schur, own, other, outer_link))
        outer_diag = outer_diag - mm(outer_link, out(own))
        outer_link = -mm(outer_link, out(other))
        inner_diag, inner_link = outer_diag, outer_link
        half *= 2

    def ends(x):
        return x[..., :1, :], x[..., SUB - 1 :, :]

    side = lax.broadcasted_iota(jnp.int32, (2, lines), 0) == 0
    unit2 = diagonal_block(jnp.ones((2, lines), jnp.float32))
    signed = jnp.where(side, 0.5, -0.5)

    def both(first, second):
        shape = first.shape[:-2] + (2, lines)
        return jnp.where(side, jnp.broadcast_to(first, shape), jnp.broadcast_to(second, shape))

    def swap2(x):
        return both(x[..., 1:, :], x[..., :1, :])

    def put(buffer, r, pieces, send, recv):
        for i, piece in enumerate(pieces):
            buffer[r, bits[r], i] = piece
        copy = remote(
            buffer.at[r, bits[r]], buffer.at[r, bits[r]], send.at[r], recv.at[r],
            (partners[r], row),
        )
        copy.start()
        return copy

    group = [
        both(*ends(outer_diag)), both(*ends(outer_link)),
        both(jac[:, :, :1, :], jac[:, :, cells - 1 :, :]),
    ]
    mat_copy = put(mats, 0, group, mat_send, mat_recv)

    for copy in halo_copies:
        copy.wait()
    tails = jnp.where(row > 0, halo_in[0].astype(jnp.float32), 0.0)
    heads = jnp.where(row < cross_size - 1, halo_in[1].astype(jnp.float32), 0.0)
    for f in range(UNK):
        field = flux[f].astype(jnp.float32)
        tail = tails if f == 0 else pltpu.roll(tails, lines - NZ * f, 1)
        head = pltpu.roll(heads, lines - NZ - NZ * f, 1)
        behind = jnp.where(lane < NZ, tail, pltpu.roll(field, NZ, 1))
        ahead = jnp.where(lane >= lines - NZ, head, pltpu.roll(field, lines - NZ, 1))
        res[f] = source[f].astype(jnp.float32) - 0.5 * (ahead - behind)

    rhs = [res[:, pl.ds(t, SUB, stride=STEPS), :] for t in range(STEPS)]
    y1 = mv(schur1, rhs[1] - mv(up12, rhs[2] * over2))
    y2 = mv(schur2, rhs[2] - mv(low21, rhs[1] * over1))
    head_rhs = rhs[0] - mv(up0, y1)
    tail_rhs = rhs[3] - mv(low3, y2)
    inner_rhs = jnp.where(even, tail_rhs, head_rhs)
    outer_rhs = jnp.where(even, head_rhs, tail_rhs)
    ys = []
    for half, left, swap, out, inv, couple, schur, own, other, link in levels:
        y = mv(schur, inner_rhs - mv(couple, swap(mv(inv, inner_rhs))))
        ys.append(y)
        outer_rhs = outer_rhs - mv(link, out(y))
        inner_rhs = outer_rhs
    ends_rhs = both(*ends(outer_rhs))

    merged = []
    for r in range(rounds - 1):
        if r > 0:
            mat_copy = put(mats, r, group, mat_send, mat_recv)
        rhs_copy = put(rhss, r, [ends_rhs], rhs_send, rhs_recv)
        mat_copy.wait()

        def inner(ref, i):
            return both(ref[r, 0, i][..., 1:, :], ref[r, 1, i][..., :1, :])

        def outer(ref, i):
            return jnp.where(side, ref[r, 0, i], ref[r, 1, i])

        couple = swap2(inner(mats, 2)) * signed - damping * unit2
        diag_in, link_in = inner(mats, 0), inner(mats, 1)
        diag_out, link_out = outer(mats, 0), outer(mats, 1)
        inv = inverse(diag_in)
        through = mm(inv, couple)
        schur = inverse(diag_in - mm(couple, swap2(through)))
        own = mm(schur, link_in)
        other = -mm(through, swap2(own))
        group = [
            diag_out - mm(link_out, own), -mm(link_out, other), outer(mats, 2),
        ]
        rhs_copy.wait()
        rhs_in = inner(rhss, 0)
        y = mv(schur, rhs_in - mv(couple, swap2(mv(inv, rhs_in))))
        ends_rhs = outer(rhss, 0) - mv(link_out, y)
        merged.append((own, other, y))

    final = rounds - 1
    is_left = bits[final] == 0
    inv = inverse(group[0])
    far = mm(inv, group[1])
    far_y = mv(inv, ends_rhs)

    def facing(x):
        return jnp.where(is_left, x[..., 1:, :], x[..., :1, :])

    mine = facing(group[0] - mm(group[1], swap2(far)))
    mine_rhs = facing(ends_rhs - mv(group[1], swap2(far_y)))
    mine_jac = facing(group[2])
    last[bits[final], :UNK] = mine
    last[bits[final], UNK : 2 * UNK] = mine_jac
    last[bits[final], 2 * UNK] = mine_rhs
    last_copy = remote(
        last.at[bits[final]], last.at[bits[final]], last_send, last_recv, (partners[final], row)
    )
    last_copy.start()
    last_copy.wait()
    theirs = 1 - bits[final]
    their_jac = last[theirs, UNK : 2 * UNK]
    unit1 = diagonal_block(jnp.ones((1, lines), jnp.float32))
    my_couple = their_jac * jnp.where(is_left, 0.5, -0.5) - damping * unit1
    their_couple = mine_jac * jnp.where(is_left, -0.5, 0.5) - damping * unit1
    inv = inverse(last[theirs, :UNK])
    meeting = solve_one(
        mine - mm(my_couple, mm(inv, their_couple)),
        mine_rhs - mv(my_couple, mv(inv, last[theirs, 2 * UNK])),
    )
    shape2 = (UNK, 2, lines)
    at_far = far_y - mv(far, jnp.broadcast_to(meeting, shape2))
    x_head = jnp.where(is_left, at_far[:, :1], meeting)
    x_tail = jnp.where(is_left, meeting, at_far[:, 1:])
    for r in reversed(range(rounds - 1)):
        own, other, y = merged[r]
        found = y - mv(own, both(x_head, x_tail)) - mv(other, both(x_tail, x_head))
        x_head, x_tail = (
            jnp.where(bits[r] == 0, x_head, found[:, 1:]),
            jnp.where(bits[r] == 0, found[:, :1], x_tail),
        )

    shape = (UNK, SUB, lines)
    current = jnp.where(
        sub < SUB // 2, jnp.broadcast_to(x_head, shape), jnp.broadcast_to(x_tail, shape)
    )
    for (half, left, swap, out, inv, couple, schur, own, other, link), y in zip(
        reversed(levels), reversed(ys)
    ):
        near = current if half == 1 else jnp.where(
            left, sub_roll(current, half - 1), sub_roll(current, 1 - half)
        )
        away = jnp.where(left, sub_roll(current, -half), sub_roll(current, half))
        found = y - mv(own, near) - mv(other, away)
        if half > 1:
            place = lax.rem(sub, 2 * half)
            current = jnp.where((place == half - 1) | (place == half), found, current)
    x0 = jnp.where(even, current, found)
    x3 = jnp.where(even, found, current)
    x1 = y1 - mv(own1, x0) - mv(other1, x3)
    x2 = y2 - mv(own2, x3) - mv(other2, x0)
    for t, value in enumerate((x0, x1, x2, x3)):
        out_ref[:, pl.ds(t, SUB, stride=STEPS), :] = value


def shards(line_size, cross_size, jacobian, time_step, source, cross_flux):
    cells, lines = time_step.shape
    rounds = line_size.bit_length() - 1
    assert line_size == 1 << rounds and rounds >= 2 and cross_size >= 3
    assert cells == SUB * STEPS
    f32, bf16 = jnp.float32, jnp.bfloat16
    dma = pltpu.SemaphoreType.DMA
    return pl.pallas_call(
        functools.partial(kernel, line_size, cross_size),
        out_shape=jax.ShapeDtypeStruct((UNK, cells, lines), f32),
        in_specs=[pl.BlockSpec(memory_space=pl.ANY)] * 4,
        out_specs=pl.BlockSpec(memory_space=pltpu.VMEM),
        scratch_shapes=[
            pltpu.VMEM((UNK, UNK, cells, lines), f32),
            pltpu.VMEM((cells, lines), f32),
            pltpu.VMEM((UNK, cells, lines), bf16),
            pltpu.VMEM((UNK, cells, lines), bf16),
            pltpu.VMEM((UNK, cells, lines), f32),
            pltpu.VMEM((2, cells, lines), bf16),
            pltpu.VMEM((2, cells, lines), bf16),
            pltpu.VMEM((rounds - 1, 2, 3, UNK, UNK, 2, lines), f32),
            pltpu.VMEM((rounds - 1, 2, 1, UNK, 2, lines), f32),
            pltpu.VMEM((2, 2 * UNK + 1, UNK, 1, lines), f32),
            dma((4,)),
            dma((2,)), dma((2,)),
            dma((rounds - 1,)), dma((rounds - 1,)),
            dma((rounds - 1,)), dma((rounds - 1,)),
            dma, dma,
        ],
        compiler_params=pltpu.CompilerParams(
            collective_id=0, has_side_effects=True, vmem_limit_bytes=32 * 1024 * 1024
        ),
        name="sweep",
    )(jacobian, time_step, source, cross_flux)


def solution(mesh):
    placed = (
        P(None, None, "line", "cross"),
        P("line", "cross"),
        P(None, "line", "cross"),
        P(None, "line", "cross"),
    )
    return jax.shard_map(
        functools.partial(shards, mesh.shape["line"], mesh.shape["cross"]),
        mesh=mesh, in_specs=placed, out_specs=P(None, "line", "cross"), check_vma=False,
    )
```

```python
import functools

import jax
import jax.numpy as jnp
from jax import lax
from jax.experimental import pallas as pl
from jax.experimental.pallas import tpu as pltpu
from jax.sharding import PartitionSpec as P

NZ = 8
UNK = 5
SUB = 8
STEPS = 4
damping = 0.05
VMEM_BYTES = 60 * 1024 * 1024
MESH = pl.DeviceIdType.MESH


def mm(matrix, operand):
    summed = matrix[:, 0][:, None] * operand[0][None]
    for k in range(1, UNK):
        summed = summed + matrix[:, k][:, None] * operand[k][None]
    return summed


def mv(matrix, vector):
    summed = matrix[:, 0] * vector[0][None]
    for k in range(1, UNK):
        summed = summed + matrix[:, k] * vector[k][None]
    return summed


def inverse(matrix):
    rows = [matrix[i] for i in range(UNK)]
    for k in range(UNK):
        pivot = rows[k]
        scale = 1.0 / pivot[k : k + 1]
        one = jnp.ones_like(scale)
        parts = [pivot[:k]] * (k > 0) + [one] + [pivot[k + 1 :]] * (k < UNK - 1)
        pivot = jnp.concatenate(parts, axis=0) * scale
        rows[k] = pivot
        for i in range(UNK):
            if i == k:
                continue
            row = rows[i]
            factor = row[k : k + 1]
            parts = [row[:k]] * (k > 0) + [jnp.zeros_like(one)] + [row[k + 1 :]] * (k < UNK - 1)
            rows[i] = jnp.concatenate(parts, axis=0) - factor * pivot
    return jnp.stack(rows, axis=0)


def solve_one(matrix, vector):
    rows = [
        jnp.concatenate([matrix[i], vector[i : i + 1]], axis=0) for i in range(UNK)
    ]
    for k in range(UNK):
        pivot = rows[k][1:] * (1.0 / rows[k][:1])
        rows[k] = pivot
        for i in range(UNK):
            if i != k:
                rows[i] = rows[i][1:] - rows[i][:1] * pivot
    return jnp.concatenate(rows, axis=0)


def diagonal_block(values):
    nothing = jnp.zeros_like(values)
    return jnp.stack(
        [jnp.stack([values if i == j else nothing for j in range(UNK)]) for i in range(UNK)]
    )


def kernel(
    line_size, cross_size,
    jac_hbm, step_hbm, source_hbm, flux_hbm, out_ref,
    jac, step, source, flux, res,
    halo_out, halo_in, mats, rhss, last,
    local_sem, halo_send, halo_recv,
    mat_send, mat_recv, rhs_send, rhs_recv, last_send, last_recv,
):
    rounds = line_size.bit_length() - 1
    me = lax.axis_index("line")
    row = lax.axis_index("cross")
    above, below = lax.rem(row + 1, cross_size), lax.rem(row + cross_size - 1, cross_size)
    bits = [lax.rem(me // (1 << r), 2) for r in range(rounds)]
    partners = [me + (1 - 2 * bits[r]) * (1 << r) for r in range(rounds)]

    barrier = pltpu.get_barrier_semaphore()
    targets = [(me, above), (me, below)] + [(partners[r], row) for r in range(rounds)]
    for target in targets:
        pl.semaphore_signal(barrier, inc=1, device_id=target, device_id_type=MESH)

    loads = [
        pltpu.make_async_copy(src, dst, local_sem.at[i])
        for i, (src, dst) in enumerate(
            [(flux_hbm, flux), (jac_hbm, jac), (step_hbm, step), (source_hbm, source)]
        )
    ]
    for load in loads:
        load.start()

    cells = jac.shape[2]
    lines = jac.shape[3]
    loads[0].wait()
    lane = lax.broadcasted_iota(jnp.int32, (cells, lines), 1)
    tails = jnp.zeros((cells, lines), jnp.float32)
    heads = jnp.zeros((cells, lines), jnp.float32)
    for f in range(UNK):
        field = flux[f].astype(jnp.float32)
        inside = (lane >= NZ * f) & (lane < NZ * (f + 1))
        tails = jnp.where(inside, pltpu.roll(field, NZ * (f + 1), 1), tails)
        heads = jnp.where(inside, field if f == 0 else pltpu.roll(field, NZ * f, 1), heads)
    halo_out[0] = tails.astype(jnp.bfloat16)
    halo_out[1] = heads.astype(jnp.bfloat16)

    def remote(src, dst, send, recv, target):
        return pltpu.make_async_remote_copy(
            src_ref=src, dst_ref=dst, send_sem=send, recv_sem=recv,
            device_id=target, device_id_type=MESH,
        )

    loads[1].wait()
    loads[2].wait()
    sub = lax.broadcasted_iota(jnp.int32, (SUB, lines), 0)
    unit = diagonal_block(jnp.ones((SUB, lines), jnp.float32))
    diag = []
    for t in range(STEPS):
        diag.append(1.0 / step[pl.ds(t, SUB, stride=STEPS), :] + 2.0 * damping)

    def jac_at(t):
        return jac[:, :, pl.ds(t, SUB, stride=STEPS), :]

    def sub_roll(values, shift):
        shift = shift % SUB
        return values if shift == 0 else pltpu.roll(values, shift, values.ndim - 2)

    def upper(block):
        return block * 0.5 - damping * unit

    def lower(block):
        return block * -0.5 - damping * unit

    over1, over2 = 1.0 / diag[1], 1.0 / diag[2]
    up12, low21 = upper(jac_at(2)), lower(jac_at(1))
    up0, low3 = upper(jac_at(1)), lower(jac_at(2))
    schur1 = inverse(diagonal_block(diag[1]) - mm(up12, low21 * over2))
    schur2 = jnp.stack([schur1[:, i] for i in range(UNK)]) * (diag[1] * over2)
    own1 = mm(schur1, lower(jac_at(0)))
    own2 = mm(schur2, upper(jac_at(3)))
    other1 = -mm(up12, own2) * over1
    other2 = -mm(low21, own1) * over2
    head_diag = diagonal_block(diag[0]) - mm(up0, own1)
    head_link = -mm(up0, other1)
    tail_diag = diagonal_block(diag[3]) - mm(low3, own2)
    tail_link = -mm(low3, other2)

    pl.semaphore_wait(barrier, len(targets))
    halo_copies = [
        remote(halo_out.at[0], halo_in.at[0], halo_send.at[0], halo_recv.at[0], (me, above)),
        remote(halo_out.at[1], halo_in.at[1], halo_send.at[1], halo_recv.at[1], (me, below)),
    ]
    for copy in halo_copies:
        copy.start()

    even = lax.rem(sub, 2) == 0
    inner_diag = jnp.where(even, tail_diag, head_diag)
    inner_link = jnp.where(even, tail_link, head_link)
    outer_diag = jnp.where(even, head_diag, tail_diag)
    outer_link = jnp.where(even, head_link, tail_link)
    to_next = upper(sub_roll(jac_at(0), -1))
    to_last = lower(sub_roll(jac_at(3), 1))
    levels = []
    half = 1
    while half < SUB:
        left = lax.rem(sub, 2 * half) < half

        def swap(x, left=left):
            return jnp.where(left, sub_roll(x, -1), sub_roll(x, 1))

        def out(x, left=left, half=half):
            return x if half == 1 else jnp.where(
                left, sub_roll(x, 1 - half), sub_roll(x, half - 1)
            )

        couple = jnp.where(left, to_next, to_last)
        inv = inverse(inner_diag)
        through = mm(inv, couple)
        schur = inverse(inner_diag - mm(couple, swap(through)))
        own = mm(schur, inner_link)
        other = -mm(through, swap(own))
        levels.append((half, left, swap, out, inv, couple, schur, own, other, outer_link))
        outer_diag = outer_diag - mm(outer_link, out(own))
        outer_link = -mm(outer_link, out(other))
        inner_diag, inner_link = outer_diag, outer_link
        half *= 2

    def ends(x):
        return x[..., :1, :], x[..., SUB - 1 :, :]

    side = lax.broadcasted_iota(jnp.int32, (2, lines), 0) == 0
    unit2 = diagonal_block(jnp.ones((2, lines), jnp.float32))
    signed = jnp.where(side, 0.5, -0.5)

    def both(first, second):
        shape = first.shape[:-2] + (2, lines)
        return jnp.where(side, jnp.broadcast_to(first, shape), jnp.broadcast_to(second, shape))

    def swap2(x):
        return both(x[..., 1:, :], x[..., :1, :])

    def put(buffer, r, pieces, send, recv):
        for i, piece in enumerate(pieces):
            buffer[r, bits[r], i] = piece
        copy = remote(
            buffer.at[r, bits[r]], buffer.at[r, bits[r]], send.at[r], recv.at[r],
            (partners[r], row),
        )
        copy.start()
        return copy

    group = [
        both(*ends(outer_diag)), both(*ends(outer_link)),
        both(jac[:, :, :1, :], jac[:, :, cells - 1 :, :]),
    ]
    mat_copy = put(mats, 0, group, mat_send, mat_recv)

    loads[3].wait()
    for copy in halo_copies:
        copy.wait()
    tails = jnp.where(row > 0, halo_in[0].astype(jnp.float32), 0.0)
    heads = jnp.where(row < cross_size - 1, halo_in[1].astype(jnp.float32), 0.0)
    for f in range(UNK):
        field = flux[f].astype(jnp.float32)
        tail = tails if f == 0 else pltpu.roll(tails, lines - NZ * f, 1)
        head = pltpu.roll(heads, lines - NZ - NZ * f, 1)
        behind = jnp.where(lane < NZ, tail, pltpu.roll(field, NZ, 1))
        ahead = jnp.where(lane >= lines - NZ, head, pltpu.roll(field, lines - NZ, 1))
        res[f] = source[f].astype(jnp.float32) - 0.5 * (ahead - behind)

    rhs = [res[:, pl.ds(t, SUB, stride=STEPS), :] for t in range(STEPS)]
    y1 = mv(schur1, rhs[1] - mv(up12, rhs[2] * over2))
    y2 = mv(schur2, rhs[2] - mv(low21, rhs[1] * over1))
    head_rhs = rhs[0] - mv(up0, y1)
    tail_rhs = rhs[3] - mv(low3, y2)
    inner_rhs = jnp.where(even, tail_rhs, head_rhs)
    outer_rhs = jnp.where(even, head_rhs, tail_rhs)
    ys = []
    for half, left, swap, out, inv, couple, schur, own, other, link in levels:
        y = mv(schur, inner_rhs - mv(couple, swap(mv(inv, inner_rhs))))
        ys.append(y)
        outer_rhs = outer_rhs - mv(link, out(y))
        inner_rhs = outer_rhs
    ends_rhs = both(*ends(outer_rhs))

    merged = []
    for r in range(rounds - 1):
        if r > 0:
            mat_copy = put(mats, r, group, mat_send, mat_recv)
        rhs_copy = put(rhss, r, [ends_rhs], rhs_send, rhs_recv)
        mat_copy.wait()

        def inner(ref, i):
            return both(ref[r, 0, i][..., 1:, :], ref[r, 1, i][..., :1, :])

        def outer(ref, i):
            return jnp.where(side, ref[r, 0, i], ref[r, 1, i])

        couple = swap2(inner(mats, 2)) * signed - damping * unit2
        diag_in, link_in = inner(mats, 0), inner(mats, 1)
        diag_out, link_out = outer(mats, 0), outer(mats, 1)
        inv = inverse(diag_in)
        through = mm(inv, couple)
        schur = inverse(diag_in - mm(couple, swap2(through)))
        own = mm(schur, link_in)
        other = -mm(through, swap2(own))
        group = [
            diag_out - mm(link_out, own), -mm(link_out, other), outer(mats, 2),
        ]
        rhs_copy.wait()
        rhs_in = inner(rhss, 0)
        y = mv(schur, rhs_in - mv(couple, swap2(mv(inv, rhs_in))))
        ends_rhs = outer(rhss, 0) - mv(link_out, y)
        merged.append((own, other, y))

    final = rounds - 1
    is_left = bits[final] == 0
    inv = inverse(group[0])
    far = mm(inv, group[1])
    far_y = mv(inv, ends_rhs)

    def facing(x):
        return jnp.where(is_left, x[..., 1:, :], x[..., :1, :])

    mine = facing(group[0] - mm(group[1], swap2(far)))
    mine_rhs = facing(ends_rhs - mv(group[1], swap2(far_y)))
    mine_jac = facing(group[2])
    last[bits[final], :UNK] = mine
    last[bits[final], UNK : 2 * UNK] = mine_jac
    last[bits[final], 2 * UNK] = mine_rhs
    last_copy = remote(
        last.at[bits[final]], last.at[bits[final]], last_send, last_recv, (partners[final], row)
    )
    last_copy.start()
    last_copy.wait()
    theirs = 1 - bits[final]
    their_jac = last[theirs, UNK : 2 * UNK]
    unit1 = diagonal_block(jnp.ones((1, lines), jnp.float32))
    my_couple = their_jac * jnp.where(is_left, 0.5, -0.5) - damping * unit1
    their_couple = mine_jac * jnp.where(is_left, -0.5, 0.5) - damping * unit1
    inv = inverse(last[theirs, :UNK])
    meeting = solve_one(
        mine - mm(my_couple, mm(inv, their_couple)),
        mine_rhs - mv(my_couple, mv(inv, last[theirs, 2 * UNK])),
    )
    shape2 = (UNK, 2, lines)
    at_far = far_y - mv(far, jnp.broadcast_to(meeting, shape2))
    x_head = jnp.where(is_left, at_far[:, :1], meeting)
    x_tail = jnp.where(is_left, meeting, at_far[:, 1:])
    for r in reversed(range(rounds - 1)):
        own, other, y = merged[r]
        found = y - mv(own, both(x_head, x_tail)) - mv(other, both(x_tail, x_head))
        x_head, x_tail = (
            jnp.where(bits[r] == 0, x_head, found[:, 1:]),
            jnp.where(bits[r] == 0, found[:, :1], x_tail),
        )

    shape = (UNK, SUB, lines)
    current = jnp.where(
        sub < SUB // 2, jnp.broadcast_to(x_head, shape), jnp.broadcast_to(x_tail, shape)
    )
    for (half, left, swap, out, inv, couple, schur, own, other, link), y in zip(
        reversed(levels), reversed(ys)
    ):
        near = current if half == 1 else jnp.where(
            left, sub_roll(current, half - 1), sub_roll(current, 1 - half)
        )
        away = jnp.where(left, sub_roll(current, -half), sub_roll(current, half))
        found = y - mv(own, near) - mv(other, away)
        if half > 1:
            place = lax.rem(sub, 2 * half)
            current = jnp.where((place == half - 1) | (place == half), found, current)
    x0 = jnp.where(even, current, found)
    x3 = jnp.where(even, found, current)
    x1 = y1 - mv(own1, x0) - mv(other1, x3)
    x2 = y2 - mv(own2, x3) - mv(other2, x0)
    for t, value in enumerate((x0, x1, x2, x3)):
        out_ref[:, pl.ds(t, SUB, stride=STEPS), :] = value


def shards(line_size, cross_size, jacobian, time_step, source, cross_flux):
    cells, lines = time_step.shape
    rounds = line_size.bit_length() - 1
    assert line_size == 1 << rounds and rounds >= 2 and cross_size >= 3
    assert cells == SUB * STEPS
    f32, bf16 = jnp.float32, jnp.bfloat16
    dma = pltpu.SemaphoreType.DMA
    return pl.pallas_call(
        functools.partial(kernel, line_size, cross_size),
        out_shape=jax.ShapeDtypeStruct((UNK, cells, lines), f32),
        in_specs=[pl.BlockSpec(memory_space=pl.ANY)] * 4,
        out_specs=pl.BlockSpec(memory_space=pltpu.VMEM),
        scratch_shapes=[
            pltpu.VMEM((UNK, UNK, cells, lines), f32),
            pltpu.VMEM((cells, lines), f32),
            pltpu.VMEM((UNK, cells, lines), bf16),
            pltpu.VMEM((UNK, cells, lines), bf16),
            pltpu.VMEM((UNK, cells, lines), f32),
            pltpu.VMEM((2, cells, lines), bf16),
            pltpu.VMEM((2, cells, lines), bf16),
            pltpu.VMEM((rounds - 1, 2, 3, UNK, UNK, 2, lines), f32),
            pltpu.VMEM((rounds - 1, 2, 1, UNK, 2, lines), f32),
            pltpu.VMEM((2, 2 * UNK + 1, UNK, 1, lines), f32),
            dma((4,)),
            dma((2,)), dma((2,)),
            dma((rounds - 1,)), dma((rounds - 1,)),
            dma((rounds - 1,)), dma((rounds - 1,)),
            dma, dma,
        ],
        compiler_params=pltpu.CompilerParams(
            collective_id=0, has_side_effects=True, vmem_limit_bytes=VMEM_BYTES
        ),
        name="sweep",
    )(jacobian, time_step, source, cross_flux)


def solution(mesh):
    placed = (
        P(None, None, "line", "cross"),
        P("line", "cross"),
        P(None, "line", "cross"),
        P(None, "line", "cross"),
    )
    return jax.shard_map(
        functools.partial(shards, mesh.shape["line"], mesh.shape["cross"]),
        mesh=mesh, in_specs=placed, out_specs=P(None, "line", "cross"), check_vma=False,
    )
```

```python
import functools

import jax
import jax.numpy as jnp
from jax import lax
from jax.experimental import pallas as pl
from jax.experimental.pallas import tpu as pltpu
from jax.sharding import PartitionSpec as P

NZ = 8
UNK = 5
SUB = 8
STEPS = 4
damping = 0.05
VMEM_BYTES = 60 * 1024 * 1024
MESH = pl.DeviceIdType.MESH


def mm(matrix, operand):
    summed = matrix[:, 0][:, None] * operand[0][None]
    for k in range(1, UNK):
        summed = summed + matrix[:, k][:, None] * operand[k][None]
    return summed


def mv(matrix, vector):
    summed = matrix[:, 0] * vector[0][None]
    for k in range(1, UNK):
        summed = summed + matrix[:, k] * vector[k][None]
    return summed


def inverse(matrix):
    rows = [matrix[i] for i in range(UNK)]
    for k in range(UNK):
        pivot = rows[k]
        scale = 1.0 / pivot[k : k + 1]
        one = jnp.ones_like(scale)
        parts = [pivot[:k]] * (k > 0) + [one] + [pivot[k + 1 :]] * (k < UNK - 1)
        pivot = jnp.concatenate(parts, axis=0) * scale
        rows[k] = pivot
        for i in range(UNK):
            if i == k:
                continue
            row = rows[i]
            factor = row[k : k + 1]
            parts = [row[:k]] * (k > 0) + [jnp.zeros_like(one)] + [row[k + 1 :]] * (k < UNK - 1)
            rows[i] = jnp.concatenate(parts, axis=0) - factor * pivot
    return jnp.stack(rows, axis=0)


def solve_one(matrix, vector):
    rows = [
        jnp.concatenate([matrix[i], vector[i : i + 1]], axis=0) for i in range(UNK)
    ]
    for k in range(UNK):
        pivot = rows[k][1:] * (1.0 / rows[k][:1])
        rows[k] = pivot
        for i in range(UNK):
            if i != k:
                rows[i] = rows[i][1:] - rows[i][:1] * pivot
    return jnp.concatenate(rows, axis=0)


def diagonal_block(values):
    nothing = jnp.zeros_like(values)
    return jnp.stack(
        [jnp.stack([values if i == j else nothing for j in range(UNK)]) for i in range(UNK)]
    )


def kernel(
    line_size, cross_size,
    jac_hbm, step_hbm, source_hbm, flux_hbm, out_ref,
    jac, step, source, flux, res,
    halo_out, halo_in, mats, rhss, last,
    local_sem, halo_send, halo_recv,
    mat_send, mat_recv, rhs_send, rhs_recv, last_send, last_recv,
):
    rounds = line_size.bit_length() - 1
    me = lax.axis_index("line")
    row = lax.axis_index("cross")
    above, below = lax.rem(row + 1, cross_size), lax.rem(row + cross_size - 1, cross_size)
    bits = [lax.rem(me // (1 << r), 2) for r in range(rounds)]
    partners = [me + (1 - 2 * bits[r]) * (1 << r) for r in range(rounds)]

    barrier = pltpu.get_barrier_semaphore()
    targets = [(me, above), (me, below)] + [(partners[r], row) for r in range(rounds)]
    for target in targets:
        pl.semaphore_signal(barrier, inc=1, device_id=target, device_id_type=MESH)

    loads = [
        pltpu.make_async_copy(src, dst, local_sem.at[i])
        for i, (src, dst) in enumerate(
            [(flux_hbm, flux), (jac_hbm, jac), (step_hbm, step), (source_hbm, source)]
        )
    ]
    for load in loads:
        load.start()

    cells = jac.shape[2]
    lines = jac.shape[3]
    loads[0].wait()
    lane = lax.broadcasted_iota(jnp.int32, (cells, lines), 1)
    tails = jnp.zeros((cells, lines), jnp.float32)
    heads = jnp.zeros((cells, lines), jnp.float32)
    for f in range(UNK):
        field = flux[f].astype(jnp.float32)
        inside = (lane >= NZ * f) & (lane < NZ * (f + 1))
        tails = jnp.where(inside, pltpu.roll(field, NZ * (f + 1), 1), tails)
        heads = jnp.where(inside, field if f == 0 else pltpu.roll(field, NZ * f, 1), heads)
    halo_out[0] = tails.astype(jnp.bfloat16)
    halo_out[1] = heads.astype(jnp.bfloat16)

    def remote(src, dst, send, recv, target):
        return pltpu.make_async_remote_copy(
            src_ref=src, dst_ref=dst, send_sem=send, recv_sem=recv,
            device_id=target, device_id_type=MESH,
        )

    loads[1].wait()
    loads[2].wait()
    sub = lax.broadcasted_iota(jnp.int32, (SUB, lines), 0)
    unit = diagonal_block(jnp.ones((SUB, lines), jnp.float32))
    diag = []
    for t in range(STEPS):
        diag.append(1.0 / step[pl.ds(t, SUB, stride=STEPS), :] + 2.0 * damping)

    def jac_at(t):
        return jac[:, :, pl.ds(t, SUB, stride=STEPS), :]

    def sub_roll(values, shift):
        shift = shift % SUB
        return values if shift == 0 else pltpu.roll(values, shift, values.ndim - 2)

    def upper(block):
        return block * 0.5 - damping * unit

    def lower(block):
        return block * -0.5 - damping * unit

    over1, over2 = 1.0 / diag[1], 1.0 / diag[2]
    up12, low21 = upper(jac_at(2)), lower(jac_at(1))
    up0, low3 = upper(jac_at(1)), lower(jac_at(2))
    schur1 = inverse(diagonal_block(diag[1]) - mm(up12, low21 * over2))
    schur2 = jnp.stack([schur1[:, i] for i in range(UNK)]) * (diag[1] * over2)
    own1 = mm(schur1, lower(jac_at(0)))
    own2 = mm(schur2, upper(jac_at(3)))
    other1 = -mm(up12, own2) * over1
    other2 = -mm(low21, own1) * over2
    head_diag = diagonal_block(diag[0]) - mm(up0, own1)
    head_link = -mm(up0, other1)
    tail_diag = diagonal_block(diag[3]) - mm(low3, own2)
    tail_link = -mm(low3, other2)

    pl.semaphore_wait(barrier, len(targets))
    halo_copies = [
        remote(halo_out.at[0], halo_in.at[0], halo_send.at[0], halo_recv.at[0], (me, above)),
        remote(halo_out.at[1], halo_in.at[1], halo_send.at[1], halo_recv.at[1], (me, below)),
    ]
    for copy in halo_copies:
        copy.start()

    even = lax.rem(sub, 2) == 0
    inner_diag = jnp.where(even, tail_diag, head_diag)
    inner_link = jnp.where(even, tail_link, head_link)
    outer_diag = jnp.where(even, head_diag, tail_diag)
    outer_link = jnp.where(even, head_link, tail_link)
    to_next = upper(sub_roll(jac_at(0), -1))
    to_last = lower(sub_roll(jac_at(3), 1))
    levels = []
    half = 1
    while half < SUB:
        left = lax.rem(sub, 2 * half) < half

        def swap(x, left=left):
            return jnp.where(left, sub_roll(x, -1), sub_roll(x, 1))

        def out(x, left=left, half=half):
            return x if half == 1 else jnp.where(
                left, sub_roll(x, 1 - half), sub_roll(x, half - 1)
            )

        couple = jnp.where(left, to_next, to_last)
        inv = inverse(inner_diag)
        through = mm(inv, couple)
        schur = inverse(inner_diag - mm(couple, swap(through)))
        own = mm(schur, inner_link)
        other = -mm(through, swap(own))
        levels.append((half, left, swap, out, inv, couple, schur, own, other, outer_link))
        outer_diag = outer_diag - mm(outer_link, out(own))
        outer_link = -mm(outer_link, out(other))
        inner_diag, inner_link = outer_diag, outer_link
        half *= 2

    def ends(x):
        return x[..., :1, :], x[..., SUB - 1 :, :]

    side = lax.broadcasted_iota(jnp.int32, (2, lines), 0) == 0
    unit2 = diagonal_block(jnp.ones((2, lines), jnp.float32))
    signed = jnp.where(side, 0.5, -0.5)

    def both(first, second):
        shape = first.shape[:-2] + (2, lines)
        return jnp.where(side, jnp.broadcast_to(first, shape), jnp.broadcast_to(second, shape))

    def swap2(x):
        return both(x[..., 1:, :], x[..., :1, :])

    def put(buffer, r, pieces, send, recv):
        for i, piece in enumerate(pieces):
            buffer[r, bits[r], i] = piece
        copy = remote(
            buffer.at[r, bits[r]], buffer.at[r, bits[r]], send.at[r], recv.at[r],
            (partners[r], row),
        )
        copy.start()
        return copy

    group = [
        both(*ends(outer_diag)), both(*ends(outer_link)),
        both(jac[:, :, :1, :], jac[:, :, cells - 1 :, :]),
    ]
    mat_copy = put(mats, 0, group, mat_send, mat_recv)

    loads[3].wait()
    for copy in halo_copies:
        copy.wait()
    tails = jnp.where(row > 0, halo_in[0].astype(jnp.float32), 0.0)
    heads = jnp.where(row < cross_size - 1, halo_in[1].astype(jnp.float32), 0.0)
    for f in range(UNK):
        field = flux[f].astype(jnp.float32)
        tail = tails if f == 0 else pltpu.roll(tails, lines - NZ * f, 1)
        head = pltpu.roll(heads, lines - NZ - NZ * f, 1)
        behind = jnp.where(lane < NZ, tail, pltpu.roll(field, NZ, 1))
        ahead = jnp.where(lane >= lines - NZ, head, pltpu.roll(field, lines - NZ, 1))
        res[f] = source[f].astype(jnp.float32) - 0.5 * (ahead - behind)

    rhs = [res[:, pl.ds(t, SUB, stride=STEPS), :] for t in range(STEPS)]
    y1 = mv(schur1, rhs[1] - mv(up12, rhs[2] * over2))
    y2 = mv(schur2, rhs[2] - mv(low21, rhs[1] * over1))
    head_rhs = rhs[0] - mv(up0, y1)
    tail_rhs = rhs[3] - mv(low3, y2)
    inner_rhs = jnp.where(even, tail_rhs, head_rhs)
    outer_rhs = jnp.where(even, head_rhs, tail_rhs)
    ys = []
    for half, left, swap, out, inv, couple, schur, own, other, link in levels:
        y = mv(schur, inner_rhs - mv(couple, swap(mv(inv, inner_rhs))))
        ys.append(y)
        outer_rhs = outer_rhs - mv(link, out(y))
        inner_rhs = outer_rhs
    ends_rhs = both(*ends(outer_rhs))

    merged = []
    for r in range(rounds - 1):
        if r > 0:
            mat_copy = put(mats, r, group, mat_send, mat_recv)
        rhs_copy = put(rhss, r, [ends_rhs], rhs_send, rhs_recv)
        mat_copy.wait()

        def inner(ref, i):
            return both(ref[r, 0, i][..., 1:, :], ref[r, 1, i][..., :1, :])

        def outer(ref, i):
            return jnp.where(side, ref[r, 0, i], ref[r, 1, i])

        couple = swap2(inner(mats, 2)) * signed - damping * unit2
        diag_in, link_in = inner(mats, 0), inner(mats, 1)
        diag_out, link_out = outer(mats, 0), outer(mats, 1)
        inv = inverse(diag_in)
        through = mm(inv, couple)
        schur = inverse(diag_in - mm(couple, swap2(through)))
        own = mm(schur, link_in)
        other = -mm(through, swap2(own))
        group = [
            diag_out - mm(link_out, own), -mm(link_out, other), outer(mats, 2),
        ]
        rhs_copy.wait()
        rhs_in = inner(rhss, 0)
        y = mv(schur, rhs_in - mv(couple, swap2(mv(inv, rhs_in))))
        ends_rhs = outer(rhss, 0) - mv(link_out, y)
        merged.append((own, other, y))

    final = rounds - 1
    is_left = bits[final] == 0
    inv = inverse(group[0])
    far = mm(inv, group[1])
    far_y = mv(inv, ends_rhs)

    def facing(x):
        return jnp.where(is_left, x[..., 1:, :], x[..., :1, :])

    mine = facing(group[0] - mm(group[1], swap2(far)))
    mine_rhs = facing(ends_rhs - mv(group[1], swap2(far_y)))
    mine_jac = facing(group[2])
    last[bits[final], :UNK] = mine
    last[bits[final], UNK : 2 * UNK] = mine_jac
    last[bits[final], 2 * UNK] = mine_rhs
    last_copy = remote(
        last.at[bits[final]], last.at[bits[final]], last_send, last_recv, (partners[final], row)
    )
    last_copy.start()
    last_copy.wait()
    theirs = 1 - bits[final]
    their_jac = last[theirs, UNK : 2 * UNK]
    unit1 = diagonal_block(jnp.ones((1, lines), jnp.float32))
    my_couple = their_jac * jnp.where(is_left, 0.5, -0.5) - damping * unit1
    their_couple = mine_jac * jnp.where(is_left, -0.5, 0.5) - damping * unit1
    inv = inverse(last[theirs, :UNK])
    meeting = solve_one(
        mine - mm(my_couple, mm(inv, their_couple)),
        mine_rhs - mv(my_couple, mv(inv, last[theirs, 2 * UNK])),
    )
    shape2 = (UNK, 2, lines)
    at_far = far_y - mv(far, jnp.broadcast_to(meeting, shape2))
    x_head = jnp.where(is_left, at_far[:, :1], meeting)
    x_tail = jnp.where(is_left, meeting, at_far[:, 1:])
    for r in reversed(range(rounds - 1)):
        own, other, y = merged[r]
        found = y - mv(own, both(x_head, x_tail)) - mv(other, both(x_tail, x_head))
        x_head, x_tail = (
            jnp.where(bits[r] == 0, x_head, found[:, 1:]),
            jnp.where(bits[r] == 0, found[:, :1], x_tail),
        )

    shape = (UNK, SUB, lines)
    current = jnp.where(
        sub < SUB // 2, jnp.broadcast_to(x_head, shape), jnp.broadcast_to(x_tail, shape)
    )
    for (half, left, swap, out, inv, couple, schur, own, other, link), y in zip(
        reversed(levels), reversed(ys)
    ):
        near = current if half == 1 else jnp.where(
            left, sub_roll(current, half - 1), sub_roll(current, 1 - half)
        )
        away = jnp.where(left, sub_roll(current, -half), sub_roll(current, half))
        found = y - mv(own, near) - mv(other, away)
        if half > 1:
            place = lax.rem(sub, 2 * half)
            current = jnp.where((place == half - 1) | (place == half), found, current)
    x0 = jnp.where(even, current, found)
    x3 = jnp.where(even, found, current)
    x1 = y1 - mv(own1, x0) - mv(other1, x3)
    x2 = y2 - mv(own2, x3) - mv(other2, x0)
    for t, value in enumerate((x0, x1, x2, x3)):
        out_ref[:, pl.ds(t, SUB, stride=STEPS), :] = value


def shards(line_size, cross_size, jacobian, time_step, source, cross_flux):
    cells, lines = time_step.shape
    rounds = line_size.bit_length() - 1
    assert line_size == 1 << rounds and rounds >= 2 and cross_size >= 3
    assert cells == SUB * STEPS
    f32, bf16 = jnp.float32, jnp.bfloat16
    dma = pltpu.SemaphoreType.DMA
    return pl.pallas_call(
        functools.partial(kernel, line_size, cross_size),
        out_shape=pltpu.VMEM((UNK, cells, lines), f32),
        in_specs=[pl.BlockSpec(memory_space=pl.ANY)] * 4,
        out_specs=pl.BlockSpec(memory_space=pltpu.VMEM),
        scratch_shapes=[
            pltpu.VMEM((UNK, UNK, cells, lines), f32),
            pltpu.VMEM((cells, lines), f32),
            pltpu.VMEM((UNK, cells, lines), bf16),
            pltpu.VMEM((UNK, cells, lines), bf16),
            pltpu.VMEM((UNK, cells, lines), f32),
            pltpu.VMEM((2, cells, lines), bf16),
            pltpu.VMEM((2, cells, lines), bf16),
            pltpu.VMEM((rounds - 1, 2, 3, UNK, UNK, 2, lines), f32),
            pltpu.VMEM((rounds - 1, 2, 1, UNK, 2, lines), f32),
            pltpu.VMEM((2, 2 * UNK + 1, UNK, 1, lines), f32),
            dma((4,)),
            dma((2,)), dma((2,)),
            dma((rounds - 1,)), dma((rounds - 1,)),
            dma((rounds - 1,)), dma((rounds - 1,)),
            dma, dma,
        ],
        compiler_params=pltpu.CompilerParams(
            collective_id=0, has_side_effects=True, vmem_limit_bytes=VMEM_BYTES
        ),
        name="sweep",
    )(jacobian, time_step, source, cross_flux)


def solution(mesh):
    placed = (
        P(None, None, "line", "cross"),
        P("line", "cross"),
        P(None, "line", "cross"),
        P(None, "line", "cross"),
    )
    return jax.shard_map(
        functools.partial(shards, mesh.shape["line"], mesh.shape["cross"]),
        mesh=mesh, in_specs=placed, out_specs=P(None, "line", "cross"), check_vma=False,
    )
```

```python
import functools

import jax
import jax.numpy as jnp
from jax import lax
from jax.experimental import pallas as pl
from jax.experimental.pallas import tpu as pltpu
from jax.sharding import PartitionSpec as P

NZ = 8
UNK = 5
SUB = 8
STEPS = 4
damping = 0.05
VMEM_BYTES = 60 * 1024 * 1024
MESH = pl.DeviceIdType.MESH


def mm(matrix, operand):
    summed = matrix[:, 0][:, None] * operand[0][None]
    for k in range(1, UNK):
        summed = summed + matrix[:, k][:, None] * operand[k][None]
    return summed


def mv(matrix, vector):
    summed = matrix[:, 0] * vector[0][None]
    for k in range(1, UNK):
        summed = summed + matrix[:, k] * vector[k][None]
    return summed


def inverse(matrix):
    rows = [matrix[i] for i in range(UNK)]
    for k in range(UNK):
        pivot = rows[k]
        scale = 1.0 / pivot[k : k + 1]
        one = jnp.ones_like(scale)
        parts = [pivot[:k]] * (k > 0) + [one] + [pivot[k + 1 :]] * (k < UNK - 1)
        pivot = jnp.concatenate(parts, axis=0) * scale
        rows[k] = pivot
        for i in range(UNK):
            if i == k:
                continue
            row = rows[i]
            factor = row[k : k + 1]
            parts = [row[:k]] * (k > 0) + [jnp.zeros_like(one)] + [row[k + 1 :]] * (k < UNK - 1)
            rows[i] = jnp.concatenate(parts, axis=0) - factor * pivot
    return jnp.stack(rows, axis=0)


def solve_one(matrix, vector):
    rows = [
        jnp.concatenate([matrix[i], vector[i : i + 1]], axis=0) for i in range(UNK)
    ]
    for k in range(UNK):
        pivot = rows[k][1:] * (1.0 / rows[k][:1])
        rows[k] = pivot
        for i in range(UNK):
            if i != k:
                rows[i] = rows[i][1:] - rows[i][:1] * pivot
    return jnp.concatenate(rows, axis=0)


def diagonal_block(values):
    nothing = jnp.zeros_like(values)
    return jnp.stack(
        [jnp.stack([values if i == j else nothing for j in range(UNK)]) for i in range(UNK)]
    )


def kernel(
    line_size, cross_size,
    jac_hbm, step_hbm, source_hbm, flux_hbm, out_ref,
    jac, step, source, flux, res,
    halo_out, halo_in, mats, rhss, last,
    local_sem, halo_send, halo_recv,
    mat_send, mat_recv, rhs_send, rhs_recv, last_send, last_recv,
):
    rounds = line_size.bit_length() - 1
    me = lax.axis_index("line")
    row = lax.axis_index("cross")
    above, below = row + 1, row - 1
    has_above, has_below = row < cross_size - 1, row > 0
    bits = [lax.rem(me // (1 << r), 2) for r in range(rounds)]
    partners = [me + (1 - 2 * bits[r]) * (1 << r) for r in range(rounds)]

    barrier = pltpu.get_barrier_semaphore()
    def greet(target):
        pl.semaphore_signal(barrier, inc=1, device_id=target, device_id_type=MESH)

    @pl.when(has_above)
    def _():
        greet((me, above))

    @pl.when(has_below)
    def _():
        greet((me, below))

    for r in range(rounds):
        greet((partners[r], row))

    loads = [
        pltpu.make_async_copy(src, dst, local_sem.at[i])
        for i, (src, dst) in enumerate(
            [(flux_hbm, flux), (jac_hbm, jac), (step_hbm, step), (source_hbm, source)]
        )
    ]
    for load in loads:
        load.start()

    cells = jac.shape[2]
    lines = jac.shape[3]
    loads[0].wait()
    lane = lax.broadcasted_iota(jnp.int32, (cells, lines), 1)
    tails = jnp.zeros((cells, lines), jnp.float32)
    heads = jnp.zeros((cells, lines), jnp.float32)
    for f in range(UNK):
        field = flux[f].astype(jnp.float32)
        inside = (lane >= NZ * f) & (lane < NZ * (f + 1))
        tails = jnp.where(inside, pltpu.roll(field, NZ * (f + 1), 1), tails)
        heads = jnp.where(inside, field if f == 0 else pltpu.roll(field, NZ * f, 1), heads)
    halo_out[0] = tails.astype(jnp.bfloat16)
    halo_out[1] = heads.astype(jnp.bfloat16)

    def remote(src, dst, send, recv, target):
        return pltpu.make_async_remote_copy(
            src_ref=src, dst_ref=dst, send_sem=send, recv_sem=recv,
            device_id=target, device_id_type=MESH,
        )

    loads[1].wait()
    loads[2].wait()
    sub = lax.broadcasted_iota(jnp.int32, (SUB, lines), 0)
    unit = diagonal_block(jnp.ones((SUB, lines), jnp.float32))
    diag = []
    for t in range(STEPS):
        diag.append(1.0 / step[pl.ds(t, SUB, stride=STEPS), :] + 2.0 * damping)

    def jac_at(t):
        return jac[:, :, pl.ds(t, SUB, stride=STEPS), :]

    def sub_roll(values, shift):
        shift = shift % SUB
        return values if shift == 0 else pltpu.roll(values, shift, values.ndim - 2)

    def upper(block):
        return block * 0.5 - damping * unit

    def lower(block):
        return block * -0.5 - damping * unit

    over1, over2 = 1.0 / diag[1], 1.0 / diag[2]
    up12, low21 = upper(jac_at(2)), lower(jac_at(1))
    up0, low3 = upper(jac_at(1)), lower(jac_at(2))
    schur1 = inverse(diagonal_block(diag[1]) - mm(up12, low21 * over2))
    schur2 = jnp.stack([schur1[:, i] for i in range(UNK)]) * (diag[1] * over2)
    own1 = mm(schur1, lower(jac_at(0)))
    own2 = mm(schur2, upper(jac_at(3)))
    other1 = -mm(up12, own2) * over1
    other2 = -mm(low21, own1) * over2
    head_diag = diagonal_block(diag[0]) - mm(up0, own1)
    head_link = -mm(up0, other1)
    tail_diag = diagonal_block(diag[3]) - mm(low3, own2)
    tail_link = -mm(low3, other2)

    inside_rows = has_above & has_below

    @pl.when(inside_rows)
    def _():
        pl.semaphore_wait(barrier, rounds + 2)

    @pl.when(jnp.logical_not(inside_rows))
    def _():
        pl.semaphore_wait(barrier, rounds + 1)

    up_copy = remote(halo_out.at[0], halo_in.at[0], halo_send.at[0], halo_recv.at[0], (me, above))
    down_copy = remote(halo_out.at[1], halo_in.at[1], halo_send.at[1], halo_recv.at[1], (me, below))

    @pl.when(has_above)
    def _():
        up_copy.start()

    @pl.when(has_below)
    def _():
        down_copy.start()

    even = lax.rem(sub, 2) == 0
    inner_diag = jnp.where(even, tail_diag, head_diag)
    inner_link = jnp.where(even, tail_link, head_link)
    outer_diag = jnp.where(even, head_diag, tail_diag)
    outer_link = jnp.where(even, head_link, tail_link)
    to_next = upper(sub_roll(jac_at(0), -1))
    to_last = lower(sub_roll(jac_at(3), 1))
    levels = []
    half = 1
    while half < SUB:
        left = lax.rem(sub, 2 * half) < half

        def swap(x, left=left):
            return jnp.where(left, sub_roll(x, -1), sub_roll(x, 1))

        def out(x, left=left, half=half):
            return x if half == 1 else jnp.where(
                left, sub_roll(x, 1 - half), sub_roll(x, half - 1)
            )

        couple = jnp.where(left, to_next, to_last)
        inv = inverse(inner_diag)
        through = mm(inv, couple)
        schur = inverse(inner_diag - mm(couple, swap(through)))
        own = mm(schur, inner_link)
        other = -mm(through, swap(own))
        levels.append((half, left, swap, out, inv, couple, schur, own, other, outer_link))
        outer_diag = outer_diag - mm(outer_link, out(own))
        outer_link = -mm(outer_link, out(other))
        inner_diag, inner_link = outer_diag, outer_link
        half *= 2

    def ends(x):
        return x[..., :1, :], x[..., SUB - 1 :, :]

    side = lax.broadcasted_iota(jnp.int32, (2, lines), 0) == 0
    unit2 = diagonal_block(jnp.ones((2, lines), jnp.float32))
    signed = jnp.where(side, 0.5, -0.5)

    def both(first, second):
        shape = first.shape[:-2] + (2, lines)
        return jnp.where(side, jnp.broadcast_to(first, shape), jnp.broadcast_to(second, shape))

    def swap2(x):
        return both(x[..., 1:, :], x[..., :1, :])

    def put(buffer, r, pieces, send, recv):
        for i, piece in enumerate(pieces):
            buffer[r, bits[r], i] = piece
        copy = remote(
            buffer.at[r, bits[r]], buffer.at[r, bits[r]], send.at[r], recv.at[r],
            (partners[r], row),
        )
        copy.start()
        return copy

    group = [
        both(*ends(outer_diag)), both(*ends(outer_link)),
        both(jac[:, :, :1, :], jac[:, :, cells - 1 :, :]),
    ]
    mat_copy = put(mats, 0, group, mat_send, mat_recv)

    loads[3].wait()

    @pl.when(has_below)
    def _():
        up_copy.wait_recv()
        down_copy.wait_send()

    @pl.when(has_above)
    def _():
        down_copy.wait_recv()
        up_copy.wait_send()

    tails = jnp.where(has_below, halo_in[0].astype(jnp.float32), 0.0)
    heads = jnp.where(has_above, halo_in[1].astype(jnp.float32), 0.0)
    for f in range(UNK):
        field = flux[f].astype(jnp.float32)
        tail = tails if f == 0 else pltpu.roll(tails, lines - NZ * f, 1)
        head = pltpu.roll(heads, lines - NZ - NZ * f, 1)
        behind = jnp.where(lane < NZ, tail, pltpu.roll(field, NZ, 1))
        ahead = jnp.where(lane >= lines - NZ, head, pltpu.roll(field, lines - NZ, 1))
        res[f] = source[f].astype(jnp.float32) - 0.5 * (ahead - behind)

    rhs = [res[:, pl.ds(t, SUB, stride=STEPS), :] for t in range(STEPS)]
    y1 = mv(schur1, rhs[1] - mv(up12, rhs[2] * over2))
    y2 = mv(schur2, rhs[2] - mv(low21, rhs[1] * over1))
    head_rhs = rhs[0] - mv(up0, y1)
    tail_rhs = rhs[3] - mv(low3, y2)
    inner_rhs = jnp.where(even, tail_rhs, head_rhs)
    outer_rhs = jnp.where(even, head_rhs, tail_rhs)
    ys = []
    for half, left, swap, out, inv, couple, schur, own, other, link in levels:
        y = mv(schur, inner_rhs - mv(couple, swap(mv(inv, inner_rhs))))
        ys.append(y)
        outer_rhs = outer_rhs - mv(link, out(y))
        inner_rhs = outer_rhs
    ends_rhs = both(*ends(outer_rhs))

    merged = []
    for r in range(rounds - 1):
        if r > 0:
            mat_copy = put(mats, r, group, mat_send, mat_recv)
        rhs_copy = put(rhss, r, [ends_rhs], rhs_send, rhs_recv)
        mat_copy.wait()

        def inner(ref, i):
            return both(ref[r, 0, i][..., 1:, :], ref[r, 1, i][..., :1, :])

        def outer(ref, i):
            return jnp.where(side, ref[r, 0, i], ref[r, 1, i])

        couple = swap2(inner(mats, 2)) * signed - damping * unit2
        diag_in, link_in = inner(mats, 0), inner(mats, 1)
        diag_out, link_out = outer(mats, 0), outer(mats, 1)
        inv = inverse(diag_in)
        through = mm(inv, couple)
        schur = inverse(diag_in - mm(couple, swap2(through)))
        own = mm(schur, link_in)
        other = -mm(through, swap2(own))
        group = [
            diag_out - mm(link_out, own), -mm(link_out, other), outer(mats, 2),
        ]
        rhs_copy.wait()
        rhs_in = inner(rhss, 0)
        y = mv(schur, rhs_in - mv(couple, swap2(mv(inv, rhs_in))))
        ends_rhs = outer(rhss, 0) - mv(link_out, y)
        merged.append((own, other, y))

    final = rounds - 1
    is_left = bits[final] == 0
    inv = inverse(group[0])
    far = mm(inv, group[1])
    far_y = mv(inv, ends_rhs)

    def facing(x):
        return jnp.where(is_left, x[..., 1:, :], x[..., :1, :])

    mine = facing(group[0] - mm(group[1], swap2(far)))
    mine_rhs = facing(ends_rhs - mv(group[1], swap2(far_y)))
    mine_jac = facing(group[2])
    last[bits[final], :UNK] = mine
    last[bits[final], UNK : 2 * UNK] = mine_jac
    last[bits[final], 2 * UNK] = mine_rhs
    last_copy = remote(
        last.at[bits[final]], last.at[bits[final]], last_send, last_recv, (partners[final], row)
    )
    last_copy.start()
    last_copy.wait()
    theirs = 1 - bits[final]
    their_jac = last[theirs, UNK : 2 * UNK]
    unit1 = diagonal_block(jnp.ones((1, lines), jnp.float32))
    my_couple = their_jac * jnp.where(is_left, 0.5, -0.5) - damping * unit1
    their_couple = mine_jac * jnp.where(is_left, -0.5, 0.5) - damping * unit1
    inv = inverse(last[theirs, :UNK])
    meeting = solve_one(
        mine - mm(my_couple, mm(inv, their_couple)),
        mine_rhs - mv(my_couple, mv(inv, last[theirs, 2 * UNK])),
    )
    shape2 = (UNK, 2, lines)
    at_far = far_y - mv(far, jnp.broadcast_to(meeting, shape2))
    x_head = jnp.where(is_left, at_far[:, :1], meeting)
    x_tail = jnp.where(is_left, meeting, at_far[:, 1:])
    for r in reversed(range(rounds - 1)):
        own, other, y = merged[r]
        found = y - mv(own, both(x_head, x_tail)) - mv(other, both(x_tail, x_head))
        x_head, x_tail = (
            jnp.where(bits[r] == 0, x_head, found[:, 1:]),
            jnp.where(bits[r] == 0, found[:, :1], x_tail),
        )

    shape = (UNK, SUB, lines)
    current = jnp.where(
        sub < SUB // 2, jnp.broadcast_to(x_head, shape), jnp.broadcast_to(x_tail, shape)
    )
    for (half, left, swap, out, inv, couple, schur, own, other, link), y in zip(
        reversed(levels), reversed(ys)
    ):
        near = current if half == 1 else jnp.where(
            left, sub_roll(current, half - 1), sub_roll(current, 1 - half)
        )
        away = jnp.where(left, sub_roll(current, -half), sub_roll(current, half))
        found = y - mv(own, near) - mv(other, away)
        if half > 1:
            place = lax.rem(sub, 2 * half)
            current = jnp.where((place == half - 1) | (place == half), found, current)
    x0 = jnp.where(even, current, found)
    x3 = jnp.where(even, found, current)
    x1 = y1 - mv(own1, x0) - mv(other1, x3)
    x2 = y2 - mv(own2, x3) - mv(other2, x0)
    for t, value in enumerate((x0, x1, x2, x3)):
        out_ref[:, pl.ds(t, SUB, stride=STEPS), :] = value


def shards(line_size, cross_size, jacobian, time_step, source, cross_flux):
    cells, lines = time_step.shape
    rounds = line_size.bit_length() - 1
    assert line_size == 1 << rounds and rounds >= 2 and cross_size >= 3
    assert cells == SUB * STEPS
    f32, bf16 = jnp.float32, jnp.bfloat16
    dma = pltpu.SemaphoreType.DMA
    return pl.pallas_call(
        functools.partial(kernel, line_size, cross_size),
        out_shape=pltpu.VMEM((UNK, cells, lines), f32),
        in_specs=[pl.BlockSpec(memory_space=pl.ANY)] * 4,
        out_specs=pl.BlockSpec(memory_space=pltpu.VMEM),
        scratch_shapes=[
            pltpu.VMEM((UNK, UNK, cells, lines), f32),
            pltpu.VMEM((cells, lines), f32),
            pltpu.VMEM((UNK, cells, lines), bf16),
            pltpu.VMEM((UNK, cells, lines), bf16),
            pltpu.VMEM((UNK, cells, lines), f32),
            pltpu.VMEM((2, cells, lines), bf16),
            pltpu.VMEM((2, cells, lines), bf16),
            pltpu.VMEM((rounds - 1, 2, 3, UNK, UNK, 2, lines), f32),
            pltpu.VMEM((rounds - 1, 2, 1, UNK, 2, lines), f32),
            pltpu.VMEM((2, 2 * UNK + 1, UNK, 1, lines), f32),
            dma((4,)),
            dma((2,)), dma((2,)),
            dma((rounds - 1,)), dma((rounds - 1,)),
            dma((rounds - 1,)), dma((rounds - 1,)),
            dma, dma,
        ],
        compiler_params=pltpu.CompilerParams(
            collective_id=0, has_side_effects=True, vmem_limit_bytes=VMEM_BYTES
        ),
        name="sweep",
    )(jacobian, time_step, source, cross_flux)


def solution(mesh):
    placed = (
        P(None, None, "line", "cross"),
        P("line", "cross"),
        P(None, "line", "cross"),
        P(None, "line", "cross"),
    )
    return jax.shard_map(
        functools.partial(shards, mesh.shape["line"], mesh.shape["cross"]),
        mesh=mesh, in_specs=placed, out_specs=P(None, "line", "cross"), check_vma=False,
    )
```

```python
import functools

import jax
import jax.numpy as jnp
from jax import lax
from jax.experimental import pallas as pl
from jax.experimental.pallas import tpu as pltpu
from jax.sharding import PartitionSpec as P

NZ = 8
UNK = 5
SUB = 8
STEPS = 4
damping = 0.05
VMEM_BYTES = 60 * 1024 * 1024
MESH = pl.DeviceIdType.MESH


def mm(matrix, operand):
    summed = matrix[:, 0][:, None] * operand[0][None]
    for k in range(1, UNK):
        summed = summed + matrix[:, k][:, None] * operand[k][None]
    return summed


def mv(matrix, vector):
    summed = matrix[:, 0] * vector[0][None]
    for k in range(1, UNK):
        summed = summed + matrix[:, k] * vector[k][None]
    return summed


def inverse(matrix):
    rows = [matrix[i] for i in range(UNK)]
    for k in range(UNK):
        pivot = rows[k]
        scale = 1.0 / pivot[k : k + 1]
        one = jnp.ones_like(scale)
        parts = [pivot[:k]] * (k > 0) + [one] + [pivot[k + 1 :]] * (k < UNK - 1)
        pivot = jnp.concatenate(parts, axis=0) * scale
        rows[k] = pivot
        for i in range(UNK):
            if i == k:
                continue
            row = rows[i]
            factor = row[k : k + 1]
            parts = [row[:k]] * (k > 0) + [jnp.zeros_like(one)] + [row[k + 1 :]] * (k < UNK - 1)
            rows[i] = jnp.concatenate(parts, axis=0) - factor * pivot
    return jnp.stack(rows, axis=0)


def solve_one(matrix, vector):
    rows = [
        jnp.concatenate([matrix[i], vector[i : i + 1]], axis=0) for i in range(UNK)
    ]
    for k in range(UNK):
        pivot = rows[k][1:] * (1.0 / rows[k][:1])
        rows[k] = pivot
        for i in range(UNK):
            if i != k:
                rows[i] = rows[i][1:] - rows[i][:1] * pivot
    return jnp.concatenate(rows, axis=0)


def diagonal_block(values):
    nothing = jnp.zeros_like(values)
    return jnp.stack(
        [jnp.stack([values if i == j else nothing for j in range(UNK)]) for i in range(UNK)]
    )


def kernel(
    line_size, cross_size,
    jac_hbm, step_hbm, source_hbm, flux_hbm, out_ref,
    jac, step, source, flux, res,
    halo_out, halo_in, mats, rhss, last,
    local_sem, halo_send, halo_recv,
    mat_send, mat_recv, rhs_send, rhs_recv, last_send, last_recv,
):
    rounds = line_size.bit_length() - 1
    me = lax.axis_index("line")
    row = lax.axis_index("cross")
    above, below = row + 1, row - 1
    has_above, has_below = row < cross_size - 1, row > 0
    bits = [lax.rem(me // (1 << r), 2) for r in range(rounds)]
    partners = [me + (1 - 2 * bits[r]) * (1 << r) for r in range(rounds)]

    barrier = pltpu.get_barrier_semaphore()
    def greet(target):
        pl.semaphore_signal(barrier, inc=1, device_id=target, device_id_type=MESH)

    @pl.when(has_above)
    def _():
        greet((me, above))

    @pl.when(has_below)
    def _():
        greet((me, below))

    for r in range(rounds):
        greet((partners[r], row))

    loads = [
        pltpu.make_async_copy(src, dst, local_sem.at[i])
        for i, (src, dst) in enumerate(
            [(flux_hbm, flux), (jac_hbm, jac), (step_hbm, step), (source_hbm, source)]
        )
    ]
    for load in loads:
        load.start()

    cells = jac.shape[2]
    lines = jac.shape[3]
    loads[0].wait()
    lane = lax.broadcasted_iota(jnp.int32, (cells, lines), 1)
    tails = jnp.zeros((cells, lines), jnp.float32)
    heads = jnp.zeros((cells, lines), jnp.float32)
    for f in range(UNK):
        field = flux[f].astype(jnp.float32)
        inside = (lane >= NZ * f) & (lane < NZ * (f + 1))
        tails = jnp.where(inside, pltpu.roll(field, NZ * (f + 1), 1), tails)
        heads = jnp.where(inside, field if f == 0 else pltpu.roll(field, NZ * f, 1), heads)
    halo_out[0] = tails.astype(jnp.bfloat16)
    halo_out[1] = heads.astype(jnp.bfloat16)

    def remote(src, dst, send, recv, target):
        return pltpu.make_async_remote_copy(
            src_ref=src, dst_ref=dst, send_sem=send, recv_sem=recv,
            device_id=target, device_id_type=MESH,
        )

    inside_rows = has_above & has_below

    @pl.when(inside_rows)
    def _():
        pl.semaphore_wait(barrier, rounds + 2)

    @pl.when(jnp.logical_not(inside_rows))
    def _():
        pl.semaphore_wait(barrier, rounds + 1)

    up_copy = remote(halo_out.at[0], halo_in.at[0], halo_send.at[0], halo_recv.at[0], (me, above))
    down_copy = remote(halo_out.at[1], halo_in.at[1], halo_send.at[1], halo_recv.at[1], (me, below))

    @pl.when(has_above)
    def _():
        up_copy.start()

    @pl.when(has_below)
    def _():
        down_copy.start()

    loads[1].wait()
    loads[2].wait()
    sub = lax.broadcasted_iota(jnp.int32, (SUB, lines), 0)
    unit = diagonal_block(jnp.ones((SUB, lines), jnp.float32))
    diag = []
    for t in range(STEPS):
        diag.append(1.0 / step[pl.ds(t, SUB, stride=STEPS), :] + 2.0 * damping)

    def jac_at(t):
        return jac[:, :, pl.ds(t, SUB, stride=STEPS), :]

    def sub_roll(values, shift):
        shift = shift % SUB
        return values if shift == 0 else pltpu.roll(values, shift, values.ndim - 2)

    def upper(block):
        return block * 0.5 - damping * unit

    def lower(block):
        return block * -0.5 - damping * unit

    over1, over2 = 1.0 / diag[1], 1.0 / diag[2]
    up12, low21 = upper(jac_at(2)), lower(jac_at(1))
    up0, low3 = upper(jac_at(1)), lower(jac_at(2))
    schur1 = inverse(diagonal_block(diag[1]) - mm(up12, low21 * over2))
    schur2 = jnp.stack([schur1[:, i] for i in range(UNK)]) * (diag[1] * over2)
    own1 = mm(schur1, lower(jac_at(0)))
    own2 = mm(schur2, upper(jac_at(3)))
    other1 = -mm(up12, own2) * over1
    other2 = -mm(low21, own1) * over2
    head_diag = diagonal_block(diag[0]) - mm(up0, own1)
    head_link = -mm(up0, other1)
    tail_diag = diagonal_block(diag[3]) - mm(low3, own2)
    tail_link = -mm(low3, other2)

    even = lax.rem(sub, 2) == 0
    inner_diag = jnp.where(even, tail_diag, head_diag)
    inner_link = jnp.where(even, tail_link, head_link)
    outer_diag = jnp.where(even, head_diag, tail_diag)
    outer_link = jnp.where(even, head_link, tail_link)
    to_next = upper(sub_roll(jac_at(0), -1))
    to_last = lower(sub_roll(jac_at(3), 1))
    levels = []
    half = 1
    while half < SUB:
        left = lax.rem(sub, 2 * half) < half

        def swap(x, left=left):
            return jnp.where(left, sub_roll(x, -1), sub_roll(x, 1))

        def out(x, left=left, half=half):
            return x if half == 1 else jnp.where(
                left, sub_roll(x, 1 - half), sub_roll(x, half - 1)
            )

        couple = jnp.where(left, to_next, to_last)
        inv = inverse(inner_diag)
        through = mm(inv, couple)
        schur = inverse(inner_diag - mm(couple, swap(through)))
        own = mm(schur, inner_link)
        other = -mm(through, swap(own))
        levels.append((half, left, swap, out, inv, couple, schur, own, other, outer_link))
        outer_diag = outer_diag - mm(outer_link, out(own))
        outer_link = -mm(outer_link, out(other))
        inner_diag, inner_link = outer_diag, outer_link
        half *= 2

    def ends(x):
        return x[..., :1, :], x[..., SUB - 1 :, :]

    side = lax.broadcasted_iota(jnp.int32, (2, lines), 0) == 0
    unit2 = diagonal_block(jnp.ones((2, lines), jnp.float32))
    signed = jnp.where(side, 0.5, -0.5)

    def both(first, second):
        shape = first.shape[:-2] + (2, lines)
        return jnp.where(side, jnp.broadcast_to(first, shape), jnp.broadcast_to(second, shape))

    def swap2(x):
        return both(x[..., 1:, :], x[..., :1, :])

    def put(buffer, r, pieces, send, recv):
        for i, piece in enumerate(pieces):
            buffer[r, bits[r], i] = piece
        copy = remote(
            buffer.at[r, bits[r]], buffer.at[r, bits[r]], send.at[r], recv.at[r],
            (partners[r], row),
        )
        copy.start()
        return copy

    group = [
        both(*ends(outer_diag)), both(*ends(outer_link)),
        both(jac[:, :, :1, :], jac[:, :, cells - 1 :, :]),
    ]
    mat_copy = put(mats, 0, group, mat_send, mat_recv)

    loads[3].wait()

    @pl.when(has_below)
    def _():
        up_copy.wait_recv()
        down_copy.wait_send()

    @pl.when(has_above)
    def _():
        down_copy.wait_recv()
        up_copy.wait_send()

    tails = jnp.where(has_below, halo_in[0].astype(jnp.float32), 0.0)
    heads = jnp.where(has_above, halo_in[1].astype(jnp.float32), 0.0)
    for f in range(UNK):
        field = flux[f].astype(jnp.float32)
        tail = tails if f == 0 else pltpu.roll(tails, lines - NZ * f, 1)
        head = pltpu.roll(heads, lines - NZ - NZ * f, 1)
        behind = jnp.where(lane < NZ, tail, pltpu.roll(field, NZ, 1))
        ahead = jnp.where(lane >= lines - NZ, head, pltpu.roll(field, lines - NZ, 1))
        res[f] = source[f].astype(jnp.float32) - 0.5 * (ahead - behind)

    rhs = [res[:, pl.ds(t, SUB, stride=STEPS), :] for t in range(STEPS)]
    y1 = mv(schur1, rhs[1] - mv(up12, rhs[2] * over2))
    y2 = mv(schur2, rhs[2] - mv(low21, rhs[1] * over1))
    head_rhs = rhs[0] - mv(up0, y1)
    tail_rhs = rhs[3] - mv(low3, y2)
    inner_rhs = jnp.where(even, tail_rhs, head_rhs)
    outer_rhs = jnp.where(even, head_rhs, tail_rhs)
    ys = []
    for half, left, swap, out, inv, couple, schur, own, other, link in levels:
        y = mv(schur, inner_rhs - mv(couple, swap(mv(inv, inner_rhs))))
        ys.append(y)
        outer_rhs = outer_rhs - mv(link, out(y))
        inner_rhs = outer_rhs
    ends_rhs = both(*ends(outer_rhs))

    merged = []
    for r in range(rounds - 1):
        if r > 0:
            mat_copy = put(mats, r, group, mat_send, mat_recv)
        rhs_copy = put(rhss, r, [ends_rhs], rhs_send, rhs_recv)
        mat_copy.wait()

        def inner(ref, i):
            return both(ref[r, 0, i][..., 1:, :], ref[r, 1, i][..., :1, :])

        def outer(ref, i):
            return jnp.where(side, ref[r, 0, i], ref[r, 1, i])

        couple = swap2(inner(mats, 2)) * signed - damping * unit2
        diag_in, link_in = inner(mats, 0), inner(mats, 1)
        diag_out, link_out = outer(mats, 0), outer(mats, 1)
        inv = inverse(diag_in)
        through = mm(inv, couple)
        schur = inverse(diag_in - mm(couple, swap2(through)))
        own = mm(schur, link_in)
        other = -mm(through, swap2(own))
        group = [
            diag_out - mm(link_out, own), -mm(link_out, other), outer(mats, 2),
        ]
        rhs_copy.wait()
        rhs_in = inner(rhss, 0)
        y = mv(schur, rhs_in - mv(couple, swap2(mv(inv, rhs_in))))
        ends_rhs = outer(rhss, 0) - mv(link_out, y)
        merged.append((own, other, y))

    final = rounds - 1
    is_left = bits[final] == 0
    inv = inverse(group[0])
    far = mm(inv, group[1])
    far_y = mv(inv, ends_rhs)

    def facing(x):
        return jnp.where(is_left, x[..., 1:, :], x[..., :1, :])

    mine = facing(group[0] - mm(group[1], swap2(far)))
    mine_rhs = facing(ends_rhs - mv(group[1], swap2(far_y)))
    mine_jac = facing(group[2])
    last[bits[final], :UNK] = mine
    last[bits[final], UNK : 2 * UNK] = mine_jac
    last[bits[final], 2 * UNK] = mine_rhs
    last_copy = remote(
        last.at[bits[final]], last.at[bits[final]], last_send, last_recv, (partners[final], row)
    )
    last_copy.start()
    last_copy.wait()
    theirs = 1 - bits[final]
    their_jac = last[theirs, UNK : 2 * UNK]
    unit1 = diagonal_block(jnp.ones((1, lines), jnp.float32))
    my_couple = their_jac * jnp.where(is_left, 0.5, -0.5) - damping * unit1
    their_couple = mine_jac * jnp.where(is_left, -0.5, 0.5) - damping * unit1
    inv = inverse(last[theirs, :UNK])
    meeting = solve_one(
        mine - mm(my_couple, mm(inv, their_couple)),
        mine_rhs - mv(my_couple, mv(inv, last[theirs, 2 * UNK])),
    )
    shape2 = (UNK, 2, lines)
    at_far = far_y - mv(far, jnp.broadcast_to(meeting, shape2))
    x_head = jnp.where(is_left, at_far[:, :1], meeting)
    x_tail = jnp.where(is_left, meeting, at_far[:, 1:])
    for r in reversed(range(rounds - 1)):
        own, other, y = merged[r]
        found = y - mv(own, both(x_head, x_tail)) - mv(other, both(x_tail, x_head))
        x_head, x_tail = (
            jnp.where(bits[r] == 0, x_head, found[:, 1:]),
            jnp.where(bits[r] == 0, found[:, :1], x_tail),
        )

    shape = (UNK, SUB, lines)
    current = jnp.where(
        sub < SUB // 2, jnp.broadcast_to(x_head, shape), jnp.broadcast_to(x_tail, shape)
    )
    for (half, left, swap, out, inv, couple, schur, own, other, link), y in zip(
        reversed(levels), reversed(ys)
    ):
        near = current if half == 1 else jnp.where(
            left, sub_roll(current, half - 1), sub_roll(current, 1 - half)
        )
        away = jnp.where(left, sub_roll(current, -half), sub_roll(current, half))
        found = y - mv(own, near) - mv(other, away)
        if half > 1:
            place = lax.rem(sub, 2 * half)
            current = jnp.where((place == half - 1) | (place == half), found, current)
    x0 = jnp.where(even, current, found)
    x3 = jnp.where(even, found, current)
    x1 = y1 - mv(own1, x0) - mv(other1, x3)
    x2 = y2 - mv(own2, x3) - mv(other2, x0)
    for t, value in enumerate((x0, x1, x2, x3)):
        out_ref[:, pl.ds(t, SUB, stride=STEPS), :] = value


def shards(line_size, cross_size, jacobian, time_step, source, cross_flux):
    cells, lines = time_step.shape
    rounds = line_size.bit_length() - 1
    assert line_size == 1 << rounds and rounds >= 2 and cross_size >= 3
    assert cells == SUB * STEPS
    f32, bf16 = jnp.float32, jnp.bfloat16
    dma = pltpu.SemaphoreType.DMA
    return pl.pallas_call(
        functools.partial(kernel, line_size, cross_size),
        out_shape=pltpu.VMEM((UNK, cells, lines), f32),
        in_specs=[pl.BlockSpec(memory_space=pl.ANY)] * 4,
        out_specs=pl.BlockSpec(memory_space=pltpu.VMEM),
        scratch_shapes=[
            pltpu.VMEM((UNK, UNK, cells, lines), f32),
            pltpu.VMEM((cells, lines), f32),
            pltpu.VMEM((UNK, cells, lines), bf16),
            pltpu.VMEM((UNK, cells, lines), bf16),
            pltpu.VMEM((UNK, cells, lines), f32),
            pltpu.VMEM((2, cells, lines), bf16),
            pltpu.VMEM((2, cells, lines), bf16),
            pltpu.VMEM((rounds - 1, 2, 3, UNK, UNK, 2, lines), f32),
            pltpu.VMEM((rounds - 1, 2, 1, UNK, 2, lines), f32),
            pltpu.VMEM((2, 2 * UNK + 1, UNK, 1, lines), f32),
            dma((4,)),
            dma((2,)), dma((2,)),
            dma((rounds - 1,)), dma((rounds - 1,)),
            dma((rounds - 1,)), dma((rounds - 1,)),
            dma, dma,
        ],
        compiler_params=pltpu.CompilerParams(
            collective_id=0, has_side_effects=True, vmem_limit_bytes=VMEM_BYTES
        ),
        name="sweep",
    )(jacobian, time_step, source, cross_flux)


def solution(mesh):
    placed = (
        P(None, None, "line", "cross"),
        P("line", "cross"),
        P(None, "line", "cross"),
        P(None, "line", "cross"),
    )
    return jax.shard_map(
        functools.partial(shards, mesh.shape["line"], mesh.shape["cross"]),
        mesh=mesh, in_specs=placed, out_specs=P(None, "line", "cross"), check_vma=False,
    )
```

```python
import functools

import jax
import jax.numpy as jnp
from jax import lax
from jax.experimental import pallas as pl
from jax.experimental.pallas import tpu as pltpu
from jax.sharding import PartitionSpec as P

NZ = 8
UNK = 5
SUB = 8
STEPS = 4
damping = 0.05
VMEM_BYTES = 60 * 1024 * 1024
MESH = pl.DeviceIdType.MESH


def mm(matrix, operand):
    summed = matrix[:, 0][:, None] * operand[0][None]
    for k in range(1, UNK):
        summed = summed + matrix[:, k][:, None] * operand[k][None]
    return summed


def mv(matrix, vector):
    summed = matrix[:, 0] * vector[0][None]
    for k in range(1, UNK):
        summed = summed + matrix[:, k] * vector[k][None]
    return summed


def inverse(matrix):
    rows = [matrix[i] for i in range(UNK)]
    for k in range(UNK):
        pivot = rows[k]
        scale = 1.0 / pivot[k : k + 1]
        one = jnp.ones_like(scale)
        parts = [pivot[:k]] * (k > 0) + [one] + [pivot[k + 1 :]] * (k < UNK - 1)
        pivot = jnp.concatenate(parts, axis=0) * scale
        rows[k] = pivot
        for i in range(UNK):
            if i == k:
                continue
            row = rows[i]
            factor = row[k : k + 1]
            parts = [row[:k]] * (k > 0) + [jnp.zeros_like(one)] + [row[k + 1 :]] * (k < UNK - 1)
            rows[i] = jnp.concatenate(parts, axis=0) - factor * pivot
    return jnp.stack(rows, axis=0)


def solve_one(matrix, vector):
    rows = [
        jnp.concatenate([matrix[i], vector[i : i + 1]], axis=0) for i in range(UNK)
    ]
    for k in range(UNK):
        pivot = rows[k][1:] * (1.0 / rows[k][:1])
        rows[k] = pivot
        for i in range(UNK):
            if i != k:
                rows[i] = rows[i][1:] - rows[i][:1] * pivot
    return jnp.concatenate(rows, axis=0)


def diagonal_block(values):
    nothing = jnp.zeros_like(values)
    return jnp.stack(
        [jnp.stack([values if i == j else nothing for j in range(UNK)]) for i in range(UNK)]
    )


def kernel(
    line_size, cross_size,
    jac_hbm, step_hbm, source_hbm, flux_hbm, out_ref,
    jac, step, source, flux, res,
    halo_out, halo_in, mats, rhss, last,
    local_sem, halo_send, halo_recv,
    mat_send, mat_recv, rhs_send, rhs_recv, last_send, last_recv,
):
    rounds = line_size.bit_length() - 1
    me = lax.axis_index("line")
    row = lax.axis_index("cross")
    above, below = row + 1, row - 1
    has_above, has_below = row < cross_size - 1, row > 0
    bits = [lax.rem(me // (1 << r), 2) for r in range(rounds)]
    partners = [me + (1 - 2 * bits[r]) * (1 << r) for r in range(rounds)]

    barrier = pltpu.get_barrier_semaphore()
    def greet(target):
        pl.semaphore_signal(barrier, inc=1, device_id=target, device_id_type=MESH)

    @pl.when(has_above)
    def _():
        greet((me, above))

    @pl.when(has_below)
    def _():
        greet((me, below))

    for r in range(rounds):
        greet((partners[r], row))

    loads = [
        pltpu.make_async_copy(src, dst, local_sem.at[i])
        for i, (src, dst) in enumerate(
            [(flux_hbm, flux), (jac_hbm, jac), (step_hbm, step), (source_hbm, source)]
        )
    ]
    for load in loads:
        load.start()

    cells = jac.shape[2]
    lines = jac.shape[3]
    loads[0].wait()
    lane = lax.broadcasted_iota(jnp.int32, (cells, lines), 1)
    tails = jnp.zeros((cells, lines), jnp.float32)
    heads = jnp.zeros((cells, lines), jnp.float32)
    for f in range(UNK):
        field = flux[f].astype(jnp.float32)
        inside = (lane >= NZ * f) & (lane < NZ * (f + 1))
        tails = jnp.where(inside, pltpu.roll(field, NZ * (f + 1), 1), tails)
        heads = jnp.where(inside, field if f == 0 else pltpu.roll(field, NZ * f, 1), heads)
    halo_out[0] = tails.astype(jnp.bfloat16)
    halo_out[1] = heads.astype(jnp.bfloat16)

    def remote(src, dst, send, recv, target):
        return pltpu.make_async_remote_copy(
            src_ref=src, dst_ref=dst, send_sem=send, recv_sem=recv,
            device_id=target, device_id_type=MESH,
        )

    loads[1].wait()
    loads[2].wait()
    sub = lax.broadcasted_iota(jnp.int32, (SUB, lines), 0)
    unit = diagonal_block(jnp.ones((SUB, lines), jnp.float32))
    diag = []
    for t in range(STEPS):
        diag.append(1.0 / step[pl.ds(t, SUB, stride=STEPS), :] + 2.0 * damping)

    def jac_at(t):
        return jac[:, :, pl.ds(t, SUB, stride=STEPS), :]

    def sub_roll(values, shift):
        shift = shift % SUB
        return values if shift == 0 else pltpu.roll(values, shift, values.ndim - 2)

    def upper(block):
        return block * 0.5 - damping * unit

    def lower(block):
        return block * -0.5 - damping * unit

    over1, over2 = 1.0 / diag[1], 1.0 / diag[2]
    up12, low21 = upper(jac_at(2)), lower(jac_at(1))
    up0, low3 = upper(jac_at(1)), lower(jac_at(2))
    schur1 = inverse(diagonal_block(diag[1]) - mm(up12, low21 * over2))
    schur2 = jnp.stack([schur1[:, i] for i in range(UNK)]) * (diag[1] * over2)
    own1 = mm(schur1, lower(jac_at(0)))
    own2 = mm(schur2, upper(jac_at(3)))
    inside_rows = has_above & has_below

    @pl.when(inside_rows)
    def _():
        pl.semaphore_wait(barrier, rounds + 2)

    @pl.when(jnp.logical_not(inside_rows))
    def _():
        pl.semaphore_wait(barrier, rounds + 1)

    up_copy = remote(halo_out.at[0], halo_in.at[0], halo_send.at[0], halo_recv.at[0], (me, above))
    down_copy = remote(halo_out.at[1], halo_in.at[1], halo_send.at[1], halo_recv.at[1], (me, below))

    @pl.when(has_above)
    def _():
        up_copy.start()

    @pl.when(has_below)
    def _():
        down_copy.start()

    other1 = -mm(up12, own2) * over1
    other2 = -mm(low21, own1) * over2
    head_diag = diagonal_block(diag[0]) - mm(up0, own1)
    head_link = -mm(up0, other1)
    tail_diag = diagonal_block(diag[3]) - mm(low3, own2)
    tail_link = -mm(low3, other2)

    even = lax.rem(sub, 2) == 0
    inner_diag = jnp.where(even, tail_diag, head_diag)
    inner_link = jnp.where(even, tail_link, head_link)
    outer_diag = jnp.where(even, head_diag, tail_diag)
    outer_link = jnp.where(even, head_link, tail_link)
    to_next = upper(sub_roll(jac_at(0), -1))
    to_last = lower(sub_roll(jac_at(3), 1))
    levels = []
    half = 1
    while half < SUB:
        left = lax.rem(sub, 2 * half) < half

        def swap(x, left=left):
            return jnp.where(left, sub_roll(x, -1), sub_roll(x, 1))

        def out(x, left=left, half=half):
            return x if half == 1 else jnp.where(
                left, sub_roll(x, 1 - half), sub_roll(x, half - 1)
            )

        couple = jnp.where(left, to_next, to_last)
        inv = inverse(inner_diag)
        through = mm(inv, couple)
        schur = inverse(inner_diag - mm(couple, swap(through)))
        own = mm(schur, inner_link)
        other = -mm(through, swap(own))
        levels.append((half, left, swap, out, inv, couple, schur, own, other, outer_link))
        outer_diag = outer_diag - mm(outer_link, out(own))
        outer_link = -mm(outer_link, out(other))
        inner_diag, inner_link = outer_diag, outer_link
        half *= 2

    def ends(x):
        return x[..., :1, :], x[..., SUB - 1 :, :]

    side = lax.broadcasted_iota(jnp.int32, (2, lines), 0) == 0
    unit2 = diagonal_block(jnp.ones((2, lines), jnp.float32))
    signed = jnp.where(side, 0.5, -0.5)

    def both(first, second):
        shape = first.shape[:-2] + (2, lines)
        return jnp.where(side, jnp.broadcast_to(first, shape), jnp.broadcast_to(second, shape))

    def swap2(x):
        return both(x[..., 1:, :], x[..., :1, :])

    def put(buffer, r, pieces, send, recv):
        for i, piece in enumerate(pieces):
            buffer[r, bits[r], i] = piece
        copy = remote(
            buffer.at[r, bits[r]], buffer.at[r, bits[r]], send.at[r], recv.at[r],
            (partners[r], row),
        )
        copy.start()
        return copy

    group = [
        both(*ends(outer_diag)), both(*ends(outer_link)),
        both(jac[:, :, :1, :], jac[:, :, cells - 1 :, :]),
    ]
    mat_copy = put(mats, 0, group, mat_send, mat_recv)

    loads[3].wait()

    @pl.when(has_below)
    def _():
        up_copy.wait_recv()
        down_copy.wait_send()

    @pl.when(has_above)
    def _():
        down_copy.wait_recv()
        up_copy.wait_send()

    tails = jnp.where(has_below, halo_in[0].astype(jnp.float32), 0.0)
    heads = jnp.where(has_above, halo_in[1].astype(jnp.float32), 0.0)
    for f in range(UNK):
        field = flux[f].astype(jnp.float32)
        tail = tails if f == 0 else pltpu.roll(tails, lines - NZ * f, 1)
        head = pltpu.roll(heads, lines - NZ - NZ * f, 1)
        behind = jnp.where(lane < NZ, tail, pltpu.roll(field, NZ, 1))
        ahead = jnp.where(lane >= lines - NZ, head, pltpu.roll(field, lines - NZ, 1))
        res[f] = source[f].astype(jnp.float32) - 0.5 * (ahead - behind)

    rhs = [res[:, pl.ds(t, SUB, stride=STEPS), :] for t in range(STEPS)]
    y1 = mv(schur1, rhs[1] - mv(up12, rhs[2] * over2))
    y2 = mv(schur2, rhs[2] - mv(low21, rhs[1] * over1))
    head_rhs = rhs[0] - mv(up0, y1)
    tail_rhs = rhs[3] - mv(low3, y2)
    inner_rhs = jnp.where(even, tail_rhs, head_rhs)
    outer_rhs = jnp.where(even, head_rhs, tail_rhs)
    ys = []
    for half, left, swap, out, inv, couple, schur, own, other, link in levels:
        y = mv(schur, inner_rhs - mv(couple, swap(mv(inv, inner_rhs))))
        ys.append(y)
        outer_rhs = outer_rhs - mv(link, out(y))
        inner_rhs = outer_rhs
    ends_rhs = both(*ends(outer_rhs))

    merged = []
    for r in range(rounds - 1):
        if r > 0:
            mat_copy = put(mats, r, group, mat_send, mat_recv)
        rhs_copy = put(rhss, r, [ends_rhs], rhs_send, rhs_recv)
        mat_copy.wait()

        def inner(ref, i):
            return both(ref[r, 0, i][..., 1:, :], ref[r, 1, i][..., :1, :])

        def outer(ref, i):
            return jnp.where(side, ref[r, 0, i], ref[r, 1, i])

        couple = swap2(inner(mats, 2)) * signed - damping * unit2
        diag_in, link_in = inner(mats, 0), inner(mats, 1)
        diag_out, link_out = outer(mats, 0), outer(mats, 1)
        inv = inverse(diag_in)
        through = mm(inv, couple)
        schur = inverse(diag_in - mm(couple, swap2(through)))
        own = mm(schur, link_in)
        other = -mm(through, swap2(own))
        group = [
            diag_out - mm(link_out, own), -mm(link_out, other), outer(mats, 2),
        ]
        rhs_copy.wait()
        rhs_in = inner(rhss, 0)
        y = mv(schur, rhs_in - mv(couple, swap2(mv(inv, rhs_in))))
        ends_rhs = outer(rhss, 0) - mv(link_out, y)
        merged.append((own, other, y))

    final = rounds - 1
    is_left = bits[final] == 0
    inv = inverse(group[0])
    far = mm(inv, group[1])
    far_y = mv(inv, ends_rhs)

    def facing(x):
        return jnp.where(is_left, x[..., 1:, :], x[..., :1, :])

    mine = facing(group[0] - mm(group[1], swap2(far)))
    mine_rhs = facing(ends_rhs - mv(group[1], swap2(far_y)))
    mine_jac = facing(group[2])
    last[bits[final], :UNK] = mine
    last[bits[final], UNK : 2 * UNK] = mine_jac
    last[bits[final], 2 * UNK] = mine_rhs
    last_copy = remote(
        last.at[bits[final]], last.at[bits[final]], last_send, last_recv, (partners[final], row)
    )
    last_copy.start()

    far_end = lax.broadcasted_iota(jnp.int32, (2, lines), 0) == bits[final]
    base = jnp.where(far_end, far_y, jnp.zeros_like(far_y))
    slope = jnp.where(far_end, far, -unit2)
    for r in reversed(range(rounds - 1)):
        own, other, y = merged[r]
        found = y - mv(own, base) - mv(other, swap2(base))
        found_slope = -mm(own, slope) - mm(other, swap2(slope))
        first = bits[r] == 0

        def keep(old, new, first=first):
            return both(
                jnp.where(first, old[..., :1, :], new[..., 1:, :]),
                jnp.where(first, new[..., :1, :], old[..., 1:, :]),
            )

        base, slope = keep(base, found), keep(slope, found_slope)

    def spread(x):
        shape = x.shape[:-2] + (SUB, lines)
        return jnp.where(
            sub < SUB // 2,
            jnp.broadcast_to(x[..., :1, :], shape), jnp.broadcast_to(x[..., 1:, :], shape),
        )

    base, slope = spread(base), spread(slope)
    for (half, left, swap, out, inv, couple, schur, own, other, link), y in zip(
        reversed(levels), reversed(ys)
    ):
        def near(x, half=half, left=left):
            return x if half == 1 else jnp.where(
                left, sub_roll(x, half - 1), sub_roll(x, 1 - half)
            )

        def away(x, half=half, left=left):
            return jnp.where(left, sub_roll(x, -half), sub_roll(x, half))

        found = y - mv(own, near(base)) - mv(other, away(base))
        found_slope = -mm(own, near(slope)) - mm(other, away(slope))
        if half > 1:
            place = lax.rem(sub, 2 * half)
            filled = (place == half - 1) | (place == half)
            base = jnp.where(filled, found, base)
            slope = jnp.where(filled, found_slope, slope)
    base0, base3 = jnp.where(even, base, found), jnp.where(even, found, base)
    slope0, slope3 = jnp.where(even, slope, found_slope), jnp.where(even, found_slope, slope)
    base1 = y1 - mv(own1, base0) - mv(other1, base3)
    base2 = y2 - mv(own2, base3) - mv(other2, base0)
    slope1 = -mm(own1, slope0) - mm(other1, slope3)
    slope2 = -mm(own2, slope3) - mm(other2, slope0)

    last_copy.wait()
    theirs = 1 - bits[final]
    their_jac = last[theirs, UNK : 2 * UNK]
    unit1 = diagonal_block(jnp.ones((1, lines), jnp.float32))
    my_couple = their_jac * jnp.where(is_left, 0.5, -0.5) - damping * unit1
    their_couple = mine_jac * jnp.where(is_left, -0.5, 0.5) - damping * unit1
    inv = inverse(last[theirs, :UNK])
    meeting = solve_one(
        mine - mm(my_couple, mm(inv, their_couple)),
        mine_rhs - mv(my_couple, mv(inv, last[theirs, 2 * UNK])),
    )
    meeting = jnp.broadcast_to(meeting, (UNK, SUB, lines))
    cells_back = ((base0, slope0), (base1, slope1), (base2, slope2), (base3, slope3))
    for t, (base, slope) in enumerate(cells_back):
        out_ref[:, pl.ds(t, SUB, stride=STEPS), :] = base - mv(slope, meeting)


def shards(line_size, cross_size, jacobian, time_step, source, cross_flux):
    cells, lines = time_step.shape
    rounds = line_size.bit_length() - 1
    assert line_size == 1 << rounds and rounds >= 2 and cross_size >= 3
    assert cells == SUB * STEPS
    f32, bf16 = jnp.float32, jnp.bfloat16
    dma = pltpu.SemaphoreType.DMA
    return pl.pallas_call(
        functools.partial(kernel, line_size, cross_size),
        out_shape=pltpu.VMEM((UNK, cells, lines), f32),
        in_specs=[pl.BlockSpec(memory_space=pl.ANY)] * 4,
        out_specs=pl.BlockSpec(memory_space=pltpu.VMEM),
        scratch_shapes=[
            pltpu.VMEM((UNK, UNK, cells, lines), f32),
            pltpu.VMEM((cells, lines), f32),
            pltpu.VMEM((UNK, cells, lines), bf16),
            pltpu.VMEM((UNK, cells, lines), bf16),
            pltpu.VMEM((UNK, cells, lines), f32),
            pltpu.VMEM((2, cells, lines), bf16),
            pltpu.VMEM((2, cells, lines), bf16),
            pltpu.VMEM((rounds - 1, 2, 3, UNK, UNK, 2, lines), f32),
            pltpu.VMEM((rounds - 1, 2, 1, UNK, 2, lines), f32),
            pltpu.VMEM((2, 2 * UNK + 1, UNK, 1, lines), f32),
            dma((4,)),
            dma((2,)), dma((2,)),
            dma((rounds - 1,)), dma((rounds - 1,)),
            dma((rounds - 1,)), dma((rounds - 1,)),
            dma, dma,
        ],
        compiler_params=pltpu.CompilerParams(
            collective_id=0, has_side_effects=True, vmem_limit_bytes=VMEM_BYTES
        ),
        name="sweep",
    )(jacobian, time_step, source, cross_flux)


def solution(mesh):
    placed = (
        P(None, None, "line", "cross"),
        P("line", "cross"),
        P(None, "line", "cross"),
        P(None, "line", "cross"),
    )
    return jax.shard_map(
        functools.partial(shards, mesh.shape["line"], mesh.shape["cross"]),
        mesh=mesh, in_specs=placed, out_specs=P(None, "line", "cross"), check_vma=False,
    )
```

```python
import functools

import jax
import jax.numpy as jnp
from jax import lax
from jax.experimental import pallas as pl
from jax.experimental.pallas import tpu as pltpu
from jax.sharding import PartitionSpec as P

NZ = 8
UNK = 5
SUB = 8
STEPS = 4
damping = 0.05
VMEM_BYTES = 60 * 1024 * 1024
MESH = pl.DeviceIdType.MESH


def mm(matrix, operand):
    columns = [operand[k] for k in range(UNK)]
    rows = []
    for i in range(UNK):
        weights = matrix[i]
        summed = weights[:1] * columns[0]
        for k in range(1, UNK):
            summed = summed + weights[k : k + 1] * columns[k]
        rows.append(summed)
    return jnp.stack(rows)


def mv(matrix, vector):
    summed = matrix[:, 0] * vector[0][None]
    for k in range(1, UNK):
        summed = summed + matrix[:, k] * vector[k][None]
    return summed


def inverse(matrix):
    rows = [matrix[i] for i in range(UNK)]
    for k in range(UNK):
        pivot = rows[k]
        scale = 1.0 / pivot[k : k + 1]
        one = jnp.ones_like(scale)
        parts = [pivot[:k]] * (k > 0) + [one] + [pivot[k + 1 :]] * (k < UNK - 1)
        pivot = jnp.concatenate(parts, axis=0) * scale
        rows[k] = pivot
        for i in range(UNK):
            if i == k:
                continue
            row = rows[i]
            factor = row[k : k + 1]
            parts = [row[:k]] * (k > 0) + [jnp.zeros_like(one)] + [row[k + 1 :]] * (k < UNK - 1)
            rows[i] = jnp.concatenate(parts, axis=0) - factor * pivot
    return jnp.stack(rows, axis=0)


def solve_one(matrix, vector):
    rows = [
        jnp.concatenate([matrix[i], vector[i : i + 1]], axis=0) for i in range(UNK)
    ]
    for k in range(UNK):
        pivot = rows[k][1:] * (1.0 / rows[k][:1])
        rows[k] = pivot
        for i in range(UNK):
            if i != k:
                rows[i] = rows[i][1:] - rows[i][:1] * pivot
    return jnp.concatenate(rows, axis=0)


def diagonal_block(values):
    nothing = jnp.zeros_like(values)
    return jnp.stack(
        [jnp.stack([values if i == j else nothing for j in range(UNK)]) for i in range(UNK)]
    )


def kernel(
    line_size, cross_size,
    jac_hbm, step_hbm, source_hbm, flux_hbm, out_ref,
    jac, step, source, flux, res,
    halo_out, halo_in, mats, rhss, last,
    local_sem, halo_send, halo_recv,
    mat_send, mat_recv, rhs_send, rhs_recv, last_send, last_recv,
):
    rounds = line_size.bit_length() - 1
    me = lax.axis_index("line")
    row = lax.axis_index("cross")
    above, below = row + 1, row - 1
    has_above, has_below = row < cross_size - 1, row > 0
    bits = [lax.rem(me // (1 << r), 2) for r in range(rounds)]
    partners = [me + (1 - 2 * bits[r]) * (1 << r) for r in range(rounds)]

    barrier = pltpu.get_barrier_semaphore()
    def greet(target):
        pl.semaphore_signal(barrier, inc=1, device_id=target, device_id_type=MESH)

    @pl.when(has_above)
    def _():
        greet((me, above))

    @pl.when(has_below)
    def _():
        greet((me, below))

    for r in range(rounds):
        greet((partners[r], row))

    loads = [
        pltpu.make_async_copy(src, dst, local_sem.at[i])
        for i, (src, dst) in enumerate(
            [(flux_hbm, flux), (jac_hbm, jac), (step_hbm, step), (source_hbm, source)]
        )
    ]
    for load in loads:
        load.start()

    cells = jac.shape[2]
    lines = jac.shape[3]
    loads[0].wait()
    lane = lax.broadcasted_iota(jnp.int32, (cells, lines), 1)
    tails = jnp.zeros((cells, lines), jnp.float32)
    heads = jnp.zeros((cells, lines), jnp.float32)
    for f in range(UNK):
        field = flux[f].astype(jnp.float32)
        inside = (lane >= NZ * f) & (lane < NZ * (f + 1))
        tails = jnp.where(inside, pltpu.roll(field, NZ * (f + 1), 1), tails)
        heads = jnp.where(inside, field if f == 0 else pltpu.roll(field, NZ * f, 1), heads)
    halo_out[0] = tails.astype(jnp.bfloat16)
    halo_out[1] = heads.astype(jnp.bfloat16)

    def remote(src, dst, send, recv, target):
        return pltpu.make_async_remote_copy(
            src_ref=src, dst_ref=dst, send_sem=send, recv_sem=recv,
            device_id=target, device_id_type=MESH,
        )

    inside_rows = has_above & has_below

    @pl.when(inside_rows)
    def _():
        pl.semaphore_wait(barrier, rounds + 2)

    @pl.when(jnp.logical_not(inside_rows))
    def _():
        pl.semaphore_wait(barrier, rounds + 1)

    up_copy = remote(halo_out.at[0], halo_in.at[0], halo_send.at[0], halo_recv.at[0], (me, above))
    down_copy = remote(halo_out.at[1], halo_in.at[1], halo_send.at[1], halo_recv.at[1], (me, below))

    @pl.when(has_above)
    def _():
        up_copy.start()

    @pl.when(has_below)
    def _():
        down_copy.start()

    loads[1].wait()
    loads[2].wait()
    sub = lax.broadcasted_iota(jnp.int32, (SUB, lines), 0)
    unit = diagonal_block(jnp.ones((SUB, lines), jnp.float32))
    diag = []
    for t in range(STEPS):
        diag.append(1.0 / step[pl.ds(t, SUB, stride=STEPS), :] + 2.0 * damping)

    def jac_at(t):
        return jac[:, :, pl.ds(t, SUB, stride=STEPS), :]

    def sub_roll(values, shift):
        shift = shift % SUB
        return values if shift == 0 else pltpu.roll(values, shift, values.ndim - 2)

    def upper(block):
        return block * 0.5 - damping * unit

    def lower(block):
        return block * -0.5 - damping * unit

    over1, over2 = 1.0 / diag[1], 1.0 / diag[2]
    up12, low21 = upper(jac_at(2)), lower(jac_at(1))
    up0, low3 = upper(jac_at(1)), lower(jac_at(2))
    schur1 = inverse(diagonal_block(diag[1]) - mm(up12, low21 * over2))
    schur2 = jnp.stack([schur1[:, i] for i in range(UNK)]) * (diag[1] * over2)
    own1 = mm(schur1, lower(jac_at(0)))
    own2 = mm(schur2, upper(jac_at(3)))
    other1 = -mm(up12, own2) * over1
    other2 = -mm(low21, own1) * over2
    head_diag = diagonal_block(diag[0]) - mm(up0, own1)
    head_link = -mm(up0, other1)
    tail_diag = diagonal_block(diag[3]) - mm(low3, own2)
    tail_link = -mm(low3, other2)

    even = lax.rem(sub, 2) == 0
    inner_diag = jnp.where(even, tail_diag, head_diag)
    inner_link = jnp.where(even, tail_link, head_link)
    outer_diag = jnp.where(even, head_diag, tail_diag)
    outer_link = jnp.where(even, head_link, tail_link)
    to_next = upper(sub_roll(jac_at(0), -1))
    to_last = lower(sub_roll(jac_at(3), 1))
    levels = []
    half = 1
    while half < SUB:
        left = lax.rem(sub, 2 * half) < half

        def swap(x, left=left):
            return jnp.where(left, sub_roll(x, -1), sub_roll(x, 1))

        def out(x, left=left, half=half):
            return x if half == 1 else jnp.where(
                left, sub_roll(x, 1 - half), sub_roll(x, half - 1)
            )

        couple = jnp.where(left, to_next, to_last)
        inv = inverse(inner_diag)
        through = mm(inv, couple)
        schur = inverse(inner_diag - mm(couple, swap(through)))
        own = mm(schur, inner_link)
        other = -mm(through, swap(own))
        levels.append((half, left, swap, out, inv, couple, schur, own, other, outer_link))
        outer_diag = outer_diag - mm(outer_link, out(own))
        outer_link = -mm(outer_link, out(other))
        inner_diag, inner_link = outer_diag, outer_link
        half *= 2

    def ends(x):
        return x[..., :1, :], x[..., SUB - 1 :, :]

    side = lax.broadcasted_iota(jnp.int32, (2, lines), 0) == 0
    unit2 = diagonal_block(jnp.ones((2, lines), jnp.float32))
    signed = jnp.where(side, 0.5, -0.5)

    def both(first, second):
        shape = first.shape[:-2] + (2, lines)
        return jnp.where(side, jnp.broadcast_to(first, shape), jnp.broadcast_to(second, shape))

    def swap2(x):
        return both(x[..., 1:, :], x[..., :1, :])

    def put(buffer, r, pieces, send, recv):
        for i, piece in enumerate(pieces):
            buffer[r, bits[r], i] = piece
        copy = remote(
            buffer.at[r, bits[r]], buffer.at[r, bits[r]], send.at[r], recv.at[r],
            (partners[r], row),
        )
        copy.start()
        return copy

    group = [
        both(*ends(outer_diag)), both(*ends(outer_link)),
        both(jac[:, :, :1, :], jac[:, :, cells - 1 :, :]),
    ]
    mat_copy = put(mats, 0, group, mat_send, mat_recv)

    loads[3].wait()

    @pl.when(has_below)
    def _():
        up_copy.wait_recv()
        down_copy.wait_send()

    @pl.when(has_above)
    def _():
        down_copy.wait_recv()
        up_copy.wait_send()

    tails = jnp.where(has_below, halo_in[0].astype(jnp.float32), 0.0)
    heads = jnp.where(has_above, halo_in[1].astype(jnp.float32), 0.0)
    for f in range(UNK):
        field = flux[f].astype(jnp.float32)
        tail = tails if f == 0 else pltpu.roll(tails, lines - NZ * f, 1)
        head = pltpu.roll(heads, lines - NZ - NZ * f, 1)
        behind = jnp.where(lane < NZ, tail, pltpu.roll(field, NZ, 1))
        ahead = jnp.where(lane >= lines - NZ, head, pltpu.roll(field, lines - NZ, 1))
        res[f] = source[f].astype(jnp.float32) - 0.5 * (ahead - behind)

    rhs = [res[:, pl.ds(t, SUB, stride=STEPS), :] for t in range(STEPS)]
    y1 = mv(schur1, rhs[1] - mv(up12, rhs[2] * over2))
    y2 = mv(schur2, rhs[2] - mv(low21, rhs[1] * over1))
    head_rhs = rhs[0] - mv(up0, y1)
    tail_rhs = rhs[3] - mv(low3, y2)
    inner_rhs = jnp.where(even, tail_rhs, head_rhs)
    outer_rhs = jnp.where(even, head_rhs, tail_rhs)
    ys = []
    for half, left, swap, out, inv, couple, schur, own, other, link in levels:
        y = mv(schur, inner_rhs - mv(couple, swap(mv(inv, inner_rhs))))
        ys.append(y)
        outer_rhs = outer_rhs - mv(link, out(y))
        inner_rhs = outer_rhs
    ends_rhs = both(*ends(outer_rhs))

    merged = []
    for r in range(rounds - 1):
        if r > 0:
            mat_copy = put(mats, r, group, mat_send, mat_recv)
        rhs_copy = put(rhss, r, [ends_rhs], rhs_send, rhs_recv)
        mat_copy.wait()

        def inner(ref, i):
            return both(ref[r, 0, i][..., 1:, :], ref[r, 1, i][..., :1, :])

        def outer(ref, i):
            return jnp.where(side, ref[r, 0, i], ref[r, 1, i])

        couple = swap2(inner(mats, 2)) * signed - damping * unit2
        diag_in, link_in = inner(mats, 0), inner(mats, 1)
        diag_out, link_out = outer(mats, 0), outer(mats, 1)
        inv = inverse(diag_in)
        through = mm(inv, couple)
        schur = inverse(diag_in - mm(couple, swap2(through)))
        own = mm(schur, link_in)
        other = -mm(through, swap2(own))
        group = [
            diag_out - mm(link_out, own), -mm(link_out, other), outer(mats, 2),
        ]
        rhs_copy.wait()
        rhs_in = inner(rhss, 0)
        y = mv(schur, rhs_in - mv(couple, swap2(mv(inv, rhs_in))))
        ends_rhs = outer(rhss, 0) - mv(link_out, y)
        merged.append((own, other, y))

    final = rounds - 1
    is_left = bits[final] == 0
    inv = inverse(group[0])
    far = mm(inv, group[1])
    far_y = mv(inv, ends_rhs)

    def facing(x):
        return jnp.where(is_left, x[..., 1:, :], x[..., :1, :])

    mine = facing(group[0] - mm(group[1], swap2(far)))
    mine_rhs = facing(ends_rhs - mv(group[1], swap2(far_y)))
    mine_jac = facing(group[2])
    last[bits[final], :UNK] = mine
    last[bits[final], UNK : 2 * UNK] = mine_jac
    last[bits[final], 2 * UNK] = mine_rhs
    last_copy = remote(
        last.at[bits[final]], last.at[bits[final]], last_send, last_recv, (partners[final], row)
    )
    last_copy.start()
    last_copy.wait()
    theirs = 1 - bits[final]
    their_jac = last[theirs, UNK : 2 * UNK]
    unit1 = diagonal_block(jnp.ones((1, lines), jnp.float32))
    my_couple = their_jac * jnp.where(is_left, 0.5, -0.5) - damping * unit1
    their_couple = mine_jac * jnp.where(is_left, -0.5, 0.5) - damping * unit1
    inv = inverse(last[theirs, :UNK])
    meeting = solve_one(
        mine - mm(my_couple, mm(inv, their_couple)),
        mine_rhs - mv(my_couple, mv(inv, last[theirs, 2 * UNK])),
    )
    shape2 = (UNK, 2, lines)
    at_far = far_y - mv(far, jnp.broadcast_to(meeting, shape2))
    x_head = jnp.where(is_left, at_far[:, :1], meeting)
    x_tail = jnp.where(is_left, meeting, at_far[:, 1:])
    for r in reversed(range(rounds - 1)):
        own, other, y = merged[r]
        found = y - mv(own, both(x_head, x_tail)) - mv(other, both(x_tail, x_head))
        x_head, x_tail = (
            jnp.where(bits[r] == 0, x_head, found[:, 1:]),
            jnp.where(bits[r] == 0, found[:, :1], x_tail),
        )

    shape = (UNK, SUB, lines)
    current = jnp.where(
        sub < SUB // 2, jnp.broadcast_to(x_head, shape), jnp.broadcast_to(x_tail, shape)
    )
    for (half, left, swap, out, inv, couple, schur, own, other, link), y in zip(
        reversed(levels), reversed(ys)
    ):
        near = current if half == 1 else jnp.where(
            left, sub_roll(current, half - 1), sub_roll(current, 1 - half)
        )
        away = jnp.where(left, sub_roll(current, -half), sub_roll(current, half))
        found = y - mv(own, near) - mv(other, away)
        if half > 1:
            place = lax.rem(sub, 2 * half)
            current = jnp.where((place == half - 1) | (place == half), found, current)
    x0 = jnp.where(even, current, found)
    x3 = jnp.where(even, found, current)
    x1 = y1 - mv(own1, x0) - mv(other1, x3)
    x2 = y2 - mv(own2, x3) - mv(other2, x0)
    for t, value in enumerate((x0, x1, x2, x3)):
        out_ref[:, pl.ds(t, SUB, stride=STEPS), :] = value


def shards(line_size, cross_size, jacobian, time_step, source, cross_flux):
    cells, lines = time_step.shape
    rounds = line_size.bit_length() - 1
    assert line_size == 1 << rounds and rounds >= 2 and cross_size >= 3
    assert cells == SUB * STEPS
    f32, bf16 = jnp.float32, jnp.bfloat16
    dma = pltpu.SemaphoreType.DMA
    return pl.pallas_call(
        functools.partial(kernel, line_size, cross_size),
        out_shape=pltpu.VMEM((UNK, cells, lines), f32),
        in_specs=[pl.BlockSpec(memory_space=pl.ANY)] * 4,
        out_specs=pl.BlockSpec(memory_space=pltpu.VMEM),
        scratch_shapes=[
            pltpu.VMEM((UNK, UNK, cells, lines), f32),
            pltpu.VMEM((cells, lines), f32),
            pltpu.VMEM((UNK, cells, lines), bf16),
            pltpu.VMEM((UNK, cells, lines), bf16),
            pltpu.VMEM((UNK, cells, lines), f32),
            pltpu.VMEM((2, cells, lines), bf16),
            pltpu.VMEM((2, cells, lines), bf16),
            pltpu.VMEM((rounds - 1, 2, 3, UNK, UNK, 2, lines), f32),
            pltpu.VMEM((rounds - 1, 2, 1, UNK, 2, lines), f32),
            pltpu.VMEM((2, 2 * UNK + 1, UNK, 1, lines), f32),
            dma((4,)),
            dma((2,)), dma((2,)),
            dma((rounds - 1,)), dma((rounds - 1,)),
            dma((rounds - 1,)), dma((rounds - 1,)),
            dma, dma,
        ],
        compiler_params=pltpu.CompilerParams(
            collective_id=0, has_side_effects=True, vmem_limit_bytes=VMEM_BYTES
        ),
        name="sweep",
    )(jacobian, time_step, source, cross_flux)


def solution(mesh):
    placed = (
        P(None, None, "line", "cross"),
        P("line", "cross"),
        P(None, "line", "cross"),
        P(None, "line", "cross"),
    )
    return jax.shard_map(
        functools.partial(shards, mesh.shape["line"], mesh.shape["cross"]),
        mesh=mesh, in_specs=placed, out_specs=P(None, "line", "cross"), check_vma=False,
    )
```

```python
import functools

import jax
import jax.numpy as jnp
from jax import lax
from jax.experimental import pallas as pl
from jax.experimental.pallas import tpu as pltpu
from jax.sharding import PartitionSpec as P

NZ = 8
UNK = 5
SUB = 8
STEPS = 4
damping = 0.05
VMEM_BYTES = 60 * 1024 * 1024
MESH = pl.DeviceIdType.MESH


def mm(matrix, operand):
    summed = matrix[:, 0][:, None] * operand[0][None]
    for k in range(1, UNK):
        summed = summed + matrix[:, k][:, None] * operand[k][None]
    return summed


def mv(matrix, vector):
    summed = matrix[:, 0] * vector[0][None]
    for k in range(1, UNK):
        summed = summed + matrix[:, k] * vector[k][None]
    return summed


def inverse(matrix):
    rows = [matrix[i] for i in range(UNK)]
    one = jnp.ones_like(rows[0][:1])
    nothing = jnp.zeros_like(one)

    def with_columns(values, start, pieces):
        parts = [values[:start]] * (start > 0) + pieces
        stop = start + len(pieces)
        parts += [values[stop:]] * (stop < UNK)
        return jnp.concatenate(parts, axis=0)

    for start in (0, 2):
        p, q = rows[start], rows[start + 1]
        a, b = p[start : start + 1], p[start + 1 : start + 2]
        c, d = q[start : start + 1], q[start + 1 : start + 2]
        scale = 1.0 / (a * d - b * c)
        p = with_columns(p, start, [one, nothing])
        q = with_columns(q, start, [nothing, one])
        p, q = (d * p - b * q) * scale, (a * q - c * p) * scale
        rows[start], rows[start + 1] = p, q
        for i in range(UNK):
            if i not in (start, start + 1):
                row = rows[i]
                f, g = row[start : start + 1], row[start + 1 : start + 2]
                row = with_columns(row, start, [nothing, nothing])
                rows[i] = row - (f * p + g * q)
    k = UNK - 1
    pivot = rows[k]
    pivot = with_columns(pivot, k, [one]) * (1.0 / pivot[k:])
    rows[k] = pivot
    for i in range(k):
        rows[i] = with_columns(rows[i], k, [nothing]) - rows[i][k:] * pivot
    return jnp.stack(rows, axis=0)


def solve_one(matrix, vector):
    rows = [
        jnp.concatenate([matrix[i], vector[i : i + 1]], axis=0) for i in range(UNK)
    ]
    for k in range(UNK):
        pivot = rows[k][1:] * (1.0 / rows[k][:1])
        rows[k] = pivot
        for i in range(UNK):
            if i != k:
                rows[i] = rows[i][1:] - rows[i][:1] * pivot
    return jnp.concatenate(rows, axis=0)


def diagonal_block(values):
    nothing = jnp.zeros_like(values)
    return jnp.stack(
        [jnp.stack([values if i == j else nothing for j in range(UNK)]) for i in range(UNK)]
    )


def kernel(
    line_size, cross_size,
    jac_hbm, step_hbm, source_hbm, flux_hbm, out_ref,
    jac, step, source, flux, res,
    halo_out, halo_in, mats, rhss, last,
    local_sem, halo_send, halo_recv,
    mat_send, mat_recv, rhs_send, rhs_recv, last_send, last_recv,
):
    rounds = line_size.bit_length() - 1
    me = lax.axis_index("line")
    row = lax.axis_index("cross")
    above, below = row + 1, row - 1
    has_above, has_below = row < cross_size - 1, row > 0
    bits = [lax.rem(me // (1 << r), 2) for r in range(rounds)]
    partners = [me + (1 - 2 * bits[r]) * (1 << r) for r in range(rounds)]

    barrier = pltpu.get_barrier_semaphore()
    def greet(target):
        pl.semaphore_signal(barrier, inc=1, device_id=target, device_id_type=MESH)

    @pl.when(has_above)
    def _():
        greet((me, above))

    @pl.when(has_below)
    def _():
        greet((me, below))

    for r in range(rounds):
        greet((partners[r], row))

    loads = [
        pltpu.make_async_copy(src, dst, local_sem.at[i])
        for i, (src, dst) in enumerate(
            [(flux_hbm, flux), (jac_hbm, jac), (step_hbm, step), (source_hbm, source)]
        )
    ]
    for load in loads:
        load.start()

    cells = jac.shape[2]
    lines = jac.shape[3]
    loads[0].wait()
    lane = lax.broadcasted_iota(jnp.int32, (cells, lines), 1)
    tails = jnp.zeros((cells, lines), jnp.float32)
    heads = jnp.zeros((cells, lines), jnp.float32)
    for f in range(UNK):
        field = flux[f].astype(jnp.float32)
        inside = (lane >= NZ * f) & (lane < NZ * (f + 1))
        tails = jnp.where(inside, pltpu.roll(field, NZ * (f + 1), 1), tails)
        heads = jnp.where(inside, field if f == 0 else pltpu.roll(field, NZ * f, 1), heads)
    halo_out[0] = tails.astype(jnp.bfloat16)
    halo_out[1] = heads.astype(jnp.bfloat16)

    def remote(src, dst, send, recv, target):
        return pltpu.make_async_remote_copy(
            src_ref=src, dst_ref=dst, send_sem=send, recv_sem=recv,
            device_id=target, device_id_type=MESH,
        )

    inside_rows = has_above & has_below

    @pl.when(inside_rows)
    def _():
        pl.semaphore_wait(barrier, rounds + 2)

    @pl.when(jnp.logical_not(inside_rows))
    def _():
        pl.semaphore_wait(barrier, rounds + 1)

    up_copy = remote(halo_out.at[0], halo_in.at[0], halo_send.at[0], halo_recv.at[0], (me, above))
    down_copy = remote(halo_out.at[1], halo_in.at[1], halo_send.at[1], halo_recv.at[1], (me, below))

    @pl.when(has_above)
    def _():
        up_copy.start()

    @pl.when(has_below)
    def _():
        down_copy.start()

    loads[1].wait()
    loads[2].wait()
    sub = lax.broadcasted_iota(jnp.int32, (SUB, lines), 0)
    unit = diagonal_block(jnp.ones((SUB, lines), jnp.float32))
    diag = []
    for t in range(STEPS):
        diag.append(1.0 / step[pl.ds(t, SUB, stride=STEPS), :] + 2.0 * damping)

    def jac_at(t):
        return jac[:, :, pl.ds(t, SUB, stride=STEPS), :]

    def sub_roll(values, shift):
        shift = shift % SUB
        return values if shift == 0 else pltpu.roll(values, shift, values.ndim - 2)

    def upper(block):
        return block * 0.5 - damping * unit

    def lower(block):
        return block * -0.5 - damping * unit

    over1, over2 = 1.0 / diag[1], 1.0 / diag[2]
    up12, low21 = upper(jac_at(2)), lower(jac_at(1))
    up0, low3 = upper(jac_at(1)), lower(jac_at(2))
    schur1 = inverse(diagonal_block(diag[1]) - mm(up12, low21 * over2))
    schur2 = jnp.stack([schur1[:, i] for i in range(UNK)]) * (diag[1] * over2)
    own1 = mm(schur1, lower(jac_at(0)))
    own2 = mm(schur2, upper(jac_at(3)))
    other1 = -mm(up12, own2) * over1
    other2 = -mm(low21, own1) * over2
    head_diag = diagonal_block(diag[0]) - mm(up0, own1)
    head_link = -mm(up0, other1)
    tail_diag = diagonal_block(diag[3]) - mm(low3, own2)
    tail_link = -mm(low3, other2)

    even = lax.rem(sub, 2) == 0
    inner_diag = jnp.where(even, tail_diag, head_diag)
    inner_link = jnp.where(even, tail_link, head_link)
    outer_diag = jnp.where(even, head_diag, tail_diag)
    outer_link = jnp.where(even, head_link, tail_link)
    to_next = upper(sub_roll(jac_at(0), -1))
    to_last = lower(sub_roll(jac_at(3), 1))
    levels = []
    half = 1
    while half < SUB:
        left = lax.rem(sub, 2 * half) < half

        def swap(x, left=left):
            return jnp.where(left, sub_roll(x, -1), sub_roll(x, 1))

        def out(x, left=left, half=half):
            return x if half == 1 else jnp.where(
                left, sub_roll(x, 1 - half), sub_roll(x, half - 1)
            )

        couple = jnp.where(left, to_next, to_last)
        inv = inverse(inner_diag)
        through = mm(inv, couple)
        schur = inverse(inner_diag - mm(couple, swap(through)))
        own = mm(schur, inner_link)
        other = -mm(through, swap(own))
        levels.append((half, left, swap, out, inv, couple, schur, own, other, outer_link))
        outer_diag = outer_diag - mm(outer_link, out(own))
        outer_link = -mm(outer_link, out(other))
        inner_diag, inner_link = outer_diag, outer_link
        half *= 2

    def ends(x):
        return x[..., :1, :], x[..., SUB - 1 :, :]

    side = lax.broadcasted_iota(jnp.int32, (2, lines), 0) == 0
    unit2 = diagonal_block(jnp.ones((2, lines), jnp.float32))
    signed = jnp.where(side, 0.5, -0.5)

    def both(first, second):
        shape = first.shape[:-2] + (2, lines)
        return jnp.where(side, jnp.broadcast_to(first, shape), jnp.broadcast_to(second, shape))

    def swap2(x):
        return both(x[..., 1:, :], x[..., :1, :])

    def put(buffer, r, pieces, send, recv):
        for i, piece in enumerate(pieces):
            buffer[r, bits[r], i] = piece
        copy = remote(
            buffer.at[r, bits[r]], buffer.at[r, bits[r]], send.at[r], recv.at[r],
            (partners[r], row),
        )
        copy.start()
        return copy

    group = [
        both(*ends(outer_diag)), both(*ends(outer_link)),
        both(jac[:, :, :1, :], jac[:, :, cells - 1 :, :]),
    ]
    mat_copy = put(mats, 0, group, mat_send, mat_recv)

    loads[3].wait()

    @pl.when(has_below)
    def _():
        up_copy.wait_recv()
        down_copy.wait_send()

    @pl.when(has_above)
    def _():
        down_copy.wait_recv()
        up_copy.wait_send()

    tails = jnp.where(has_below, halo_in[0].astype(jnp.float32), 0.0)
    heads = jnp.where(has_above, halo_in[1].astype(jnp.float32), 0.0)
    for f in range(UNK):
        field = flux[f].astype(jnp.float32)
        tail = tails if f == 0 else pltpu.roll(tails, lines - NZ * f, 1)
        head = pltpu.roll(heads, lines - NZ - NZ * f, 1)
        behind = jnp.where(lane < NZ, tail, pltpu.roll(field, NZ, 1))
        ahead = jnp.where(lane >= lines - NZ, head, pltpu.roll(field, lines - NZ, 1))
        res[f] = source[f].astype(jnp.float32) - 0.5 * (ahead - behind)

    rhs = [res[:, pl.ds(t, SUB, stride=STEPS), :] for t in range(STEPS)]
    y1 = mv(schur1, rhs[1] - mv(up12, rhs[2] * over2))
    y2 = mv(schur2, rhs[2] - mv(low21, rhs[1] * over1))
    head_rhs = rhs[0] - mv(up0, y1)
    tail_rhs = rhs[3] - mv(low3, y2)
    inner_rhs = jnp.where(even, tail_rhs, head_rhs)
    outer_rhs = jnp.where(even, head_rhs, tail_rhs)
    ys = []
    for half, left, swap, out, inv, couple, schur, own, other, link in levels:
        y = mv(schur, inner_rhs - mv(couple, swap(mv(inv, inner_rhs))))
        ys.append(y)
        outer_rhs = outer_rhs - mv(link, out(y))
        inner_rhs = outer_rhs
    ends_rhs = both(*ends(outer_rhs))

    merged = []
    for r in range(rounds - 1):
        if r > 0:
            mat_copy = put(mats, r, group, mat_send, mat_recv)
        rhs_copy = put(rhss, r, [ends_rhs], rhs_send, rhs_recv)
        mat_copy.wait()

        def inner(ref, i):
            return both(ref[r, 0, i][..., 1:, :], ref[r, 1, i][..., :1, :])

        def outer(ref, i):
            return jnp.where(side, ref[r, 0, i], ref[r, 1, i])

        couple = swap2(inner(mats, 2)) * signed - damping * unit2
        diag_in, link_in = inner(mats, 0), inner(mats, 1)
        diag_out, link_out = outer(mats, 0), outer(mats, 1)
        inv = inverse(diag_in)
        through = mm(inv, couple)
        schur = inverse(diag_in - mm(couple, swap2(through)))
        own = mm(schur, link_in)
        other = -mm(through, swap2(own))
        group = [
            diag_out - mm(link_out, own), -mm(link_out, other), outer(mats, 2),
        ]
        rhs_copy.wait()
        rhs_in = inner(rhss, 0)
        y = mv(schur, rhs_in - mv(couple, swap2(mv(inv, rhs_in))))
        ends_rhs = outer(rhss, 0) - mv(link_out, y)
        merged.append((own, other, y))

    final = rounds - 1
    is_left = bits[final] == 0
    inv = inverse(group[0])
    far = mm(inv, group[1])
    far_y = mv(inv, ends_rhs)

    def facing(x):
        return jnp.where(is_left, x[..., 1:, :], x[..., :1, :])

    mine = facing(group[0] - mm(group[1], swap2(far)))
    mine_rhs = facing(ends_rhs - mv(group[1], swap2(far_y)))
    mine_jac = facing(group[2])
    last[bits[final], :UNK] = mine
    last[bits[final], UNK : 2 * UNK] = mine_jac
    last[bits[final], 2 * UNK] = mine_rhs
    last_copy = remote(
        last.at[bits[final]], last.at[bits[final]], last_send, last_recv, (partners[final], row)
    )
    last_copy.start()
    last_copy.wait()
    theirs = 1 - bits[final]
    their_jac = last[theirs, UNK : 2 * UNK]
    unit1 = diagonal_block(jnp.ones((1, lines), jnp.float32))
    my_couple = their_jac * jnp.where(is_left, 0.5, -0.5) - damping * unit1
    their_couple = mine_jac * jnp.where(is_left, -0.5, 0.5) - damping * unit1
    inv = inverse(last[theirs, :UNK])
    meeting = solve_one(
        mine - mm(my_couple, mm(inv, their_couple)),
        mine_rhs - mv(my_couple, mv(inv, last[theirs, 2 * UNK])),
    )
    shape2 = (UNK, 2, lines)
    at_far = far_y - mv(far, jnp.broadcast_to(meeting, shape2))
    x_head = jnp.where(is_left, at_far[:, :1], meeting)
    x_tail = jnp.where(is_left, meeting, at_far[:, 1:])
    for r in reversed(range(rounds - 1)):
        own, other, y = merged[r]
        found = y - mv(own, both(x_head, x_tail)) - mv(other, both(x_tail, x_head))
        x_head, x_tail = (
            jnp.where(bits[r] == 0, x_head, found[:, 1:]),
            jnp.where(bits[r] == 0, found[:, :1], x_tail),
        )

    shape = (UNK, SUB, lines)
    current = jnp.where(
        sub < SUB // 2, jnp.broadcast_to(x_head, shape), jnp.broadcast_to(x_tail, shape)
    )
    for (half, left, swap, out, inv, couple, schur, own, other, link), y in zip(
        reversed(levels), reversed(ys)
    ):
        near = current if half == 1 else jnp.where(
            left, sub_roll(current, half - 1), sub_roll(current, 1 - half)
        )
        away = jnp.where(left, sub_roll(current, -half), sub_roll(current, half))
        found = y - mv(own, near) - mv(other, away)
        if half > 1:
            place = lax.rem(sub, 2 * half)
            current = jnp.where((place == half - 1) | (place == half), found, current)
    x0 = jnp.where(even, current, found)
    x3 = jnp.where(even, found, current)
    x1 = y1 - mv(own1, x0) - mv(other1, x3)
    x2 = y2 - mv(own2, x3) - mv(other2, x0)
    for t, value in enumerate((x0, x1, x2, x3)):
        out_ref[:, pl.ds(t, SUB, stride=STEPS), :] = value


def shards(line_size, cross_size, jacobian, time_step, source, cross_flux):
    cells, lines = time_step.shape
    rounds = line_size.bit_length() - 1
    assert line_size == 1 << rounds and rounds >= 2 and cross_size >= 3
    assert cells == SUB * STEPS
    f32, bf16 = jnp.float32, jnp.bfloat16
    dma = pltpu.SemaphoreType.DMA
    return pl.pallas_call(
        functools.partial(kernel, line_size, cross_size),
        out_shape=pltpu.VMEM((UNK, cells, lines), f32),
        in_specs=[pl.BlockSpec(memory_space=pl.ANY)] * 4,
        out_specs=pl.BlockSpec(memory_space=pltpu.VMEM),
        scratch_shapes=[
            pltpu.VMEM((UNK, UNK, cells, lines), f32),
            pltpu.VMEM((cells, lines), f32),
            pltpu.VMEM((UNK, cells, lines), bf16),
            pltpu.VMEM((UNK, cells, lines), bf16),
            pltpu.VMEM((UNK, cells, lines), f32),
            pltpu.VMEM((2, cells, lines), bf16),
            pltpu.VMEM((2, cells, lines), bf16),
            pltpu.VMEM((rounds - 1, 2, 3, UNK, UNK, 2, lines), f32),
            pltpu.VMEM((rounds - 1, 2, 1, UNK, 2, lines), f32),
            pltpu.VMEM((2, 2 * UNK + 1, UNK, 1, lines), f32),
            dma((4,)),
            dma((2,)), dma((2,)),
            dma((rounds - 1,)), dma((rounds - 1,)),
            dma((rounds - 1,)), dma((rounds - 1,)),
            dma, dma,
        ],
        compiler_params=pltpu.CompilerParams(
            collective_id=0, has_side_effects=True, vmem_limit_bytes=VMEM_BYTES
        ),
        name="sweep",
    )(jacobian, time_step, source, cross_flux)


def solution(mesh):
    placed = (
        P(None, None, "line", "cross"),
        P("line", "cross"),
        P(None, "line", "cross"),
        P(None, "line", "cross"),
    )
    return jax.shard_map(
        functools.partial(shards, mesh.shape["line"], mesh.shape["cross"]),
        mesh=mesh, in_specs=placed, out_specs=P(None, "line", "cross"), check_vma=False,
    )
```

```python
import functools

import jax
import jax.numpy as jnp
from jax import lax
from jax.experimental import pallas as pl
from jax.experimental.pallas import tpu as pltpu
from jax.sharding import PartitionSpec as P

NZ = 8
UNK = 5
SUB = 8
STEPS = 4
damping = 0.05
VMEM_BYTES = 60 * 1024 * 1024
MESH = pl.DeviceIdType.MESH


def mm(matrix, operand):
    summed = matrix[:, 0][:, None] * operand[0][None]
    for k in range(1, UNK):
        summed = summed + matrix[:, k][:, None] * operand[k][None]
    return summed


def mv(matrix, vector):
    summed = matrix[:, 0] * vector[0][None]
    for k in range(1, UNK):
        summed = summed + matrix[:, k] * vector[k][None]
    return summed


def inverse(matrix):
    rows = [matrix[i] for i in range(UNK)]
    one = jnp.ones_like(rows[0][:1])
    nothing = jnp.zeros_like(one)

    def with_columns(values, start, pieces):
        parts = [values[:start]] * (start > 0) + pieces
        stop = start + len(pieces)
        parts += [values[stop:]] * (stop < UNK)
        return jnp.concatenate(parts, axis=0)

    for start in (0, 2):
        p, q = rows[start], rows[start + 1]
        a, b = p[start : start + 1], p[start + 1 : start + 2]
        c, d = q[start : start + 1], q[start + 1 : start + 2]
        scale = 1.0 / (a * d - b * c)
        p = with_columns(p, start, [one, nothing])
        q = with_columns(q, start, [nothing, one])
        p, q = (d * p - b * q) * scale, (a * q - c * p) * scale
        rows[start], rows[start + 1] = p, q
        for i in range(UNK):
            if i not in (start, start + 1):
                row = rows[i]
                f, g = row[start : start + 1], row[start + 1 : start + 2]
                row = with_columns(row, start, [nothing, nothing])
                rows[i] = row - (f * p + g * q)
    k = UNK - 1
    pivot = rows[k]
    pivot = with_columns(pivot, k, [one]) * (1.0 / pivot[k:])
    rows[k] = pivot
    for i in range(k):
        rows[i] = with_columns(rows[i], k, [nothing]) - rows[i][k:] * pivot
    return jnp.stack(rows, axis=0)


def solve_one(matrix, vector):
    rows = [
        jnp.concatenate([matrix[i], vector[i : i + 1]], axis=0) for i in range(UNK)
    ]
    for k in range(UNK):
        pivot = rows[k][1:] * (1.0 / rows[k][:1])
        rows[k] = pivot
        for i in range(UNK):
            if i != k:
                rows[i] = rows[i][1:] - rows[i][:1] * pivot
    return jnp.concatenate(rows, axis=0)


def diagonal_block(values):
    nothing = jnp.zeros_like(values)
    return jnp.stack(
        [jnp.stack([values if i == j else nothing for j in range(UNK)]) for i in range(UNK)]
    )


def kernel(
    line_size, cross_size,
    jac_hbm, step_hbm, source_hbm, flux_hbm, out_ref,
    jac, step, source, flux, res,
    halo_out, halo_in, mats, rhss, last,
    local_sem, halo_send, halo_recv,
    mat_send, mat_recv, rhs_send, rhs_recv, last_send, last_recv,
):
    rounds = line_size.bit_length() - 1
    me = lax.axis_index("line")
    row = lax.axis_index("cross")
    above, below = row + 1, row - 1
    has_above, has_below = row < cross_size - 1, row > 0
    bits = [lax.rem(me // (1 << r), 2) for r in range(rounds)]
    partners = [me + (1 - 2 * bits[r]) * (1 << r) for r in range(rounds)]

    barrier = pltpu.get_barrier_semaphore()
    def greet(target):
        pl.semaphore_signal(barrier, inc=1, device_id=target, device_id_type=MESH)

    @pl.when(has_above)
    def _():
        greet((me, above))

    @pl.when(has_below)
    def _():
        greet((me, below))

    for r in range(rounds):
        greet((partners[r], row))

    loads = [
        pltpu.make_async_copy(src, dst, local_sem.at[i])
        for i, (src, dst) in enumerate(
            [(flux_hbm, flux), (jac_hbm, jac), (step_hbm, step), (source_hbm, source)]
        )
    ]
    for load in loads:
        load.start()

    cells = jac.shape[2]
    lines = jac.shape[3]
    loads[0].wait()
    lane = lax.broadcasted_iota(jnp.int32, (cells, lines), 1)
    tails = jnp.zeros((cells, lines), jnp.float32)
    heads = jnp.zeros((cells, lines), jnp.float32)
    for f in range(UNK):
        field = flux[f].astype(jnp.float32)
        inside = (lane >= NZ * f) & (lane < NZ * (f + 1))
        tails = jnp.where(inside, pltpu.roll(field, NZ * (f + 1), 1), tails)
        heads = jnp.where(inside, field if f == 0 else pltpu.roll(field, NZ * f, 1), heads)
    halo_out[0] = tails.astype(jnp.bfloat16)
    halo_out[1] = heads.astype(jnp.bfloat16)

    def remote(src, dst, send, recv, target):
        return pltpu.make_async_remote_copy(
            src_ref=src, dst_ref=dst, send_sem=send, recv_sem=recv,
            device_id=target, device_id_type=MESH,
        )

    loads[1].wait()
    loads[2].wait()
    sub = lax.broadcasted_iota(jnp.int32, (SUB, lines), 0)
    unit = diagonal_block(jnp.ones((SUB, lines), jnp.float32))
    diag = []
    for t in range(STEPS):
        diag.append(1.0 / step[pl.ds(t, SUB, stride=STEPS), :] + 2.0 * damping)

    def jac_at(t):
        return jac[:, :, pl.ds(t, SUB, stride=STEPS), :]

    def sub_roll(values, shift):
        shift = shift % SUB
        return values if shift == 0 else pltpu.roll(values, shift, values.ndim - 2)

    def upper(block):
        return block * 0.5 - damping * unit

    def lower(block):
        return block * -0.5 - damping * unit

    over1, over2 = 1.0 / diag[1], 1.0 / diag[2]
    up12, low21 = upper(jac_at(2)), lower(jac_at(1))
    up0, low3 = upper(jac_at(1)), lower(jac_at(2))
    schur1 = inverse(diagonal_block(diag[1]) - mm(up12, low21 * over2))
    schur2 = jnp.stack([schur1[:, i] for i in range(UNK)]) * (diag[1] * over2)
    own1 = mm(schur1, lower(jac_at(0)))
    own2 = mm(schur2, upper(jac_at(3)))
    other1 = -mm(up12, own2) * over1
    other2 = -mm(low21, own1) * over2
    head_diag = diagonal_block(diag[0]) - mm(up0, own1)
    head_link = -mm(up0, other1)
    tail_diag = diagonal_block(diag[3]) - mm(low3, own2)
    tail_link = -mm(low3, other2)

    inside_rows = has_above & has_below

    @pl.when(inside_rows)
    def _():
        pl.semaphore_wait(barrier, rounds + 2)

    @pl.when(jnp.logical_not(inside_rows))
    def _():
        pl.semaphore_wait(barrier, rounds + 1)

    up_copy = remote(halo_out.at[0], halo_in.at[0], halo_send.at[0], halo_recv.at[0], (me, above))
    down_copy = remote(halo_out.at[1], halo_in.at[1], halo_send.at[1], halo_recv.at[1], (me, below))

    @pl.when(has_above)
    def _():
        up_copy.start()

    @pl.when(has_below)
    def _():
        down_copy.start()

    even = lax.rem(sub, 2) == 0
    inner_diag = jnp.where(even, tail_diag, head_diag)
    inner_link = jnp.where(even, tail_link, head_link)
    outer_diag = jnp.where(even, head_diag, tail_diag)
    outer_link = jnp.where(even, head_link, tail_link)
    to_next = upper(sub_roll(jac_at(0), -1))
    to_last = lower(sub_roll(jac_at(3), 1))
    levels = []
    half = 1
    while half < SUB:
        left = lax.rem(sub, 2 * half) < half

        def swap(x, left=left):
            return jnp.where(left, sub_roll(x, -1), sub_roll(x, 1))

        def out(x, left=left, half=half):
            return x if half == 1 else jnp.where(
                left, sub_roll(x, 1 - half), sub_roll(x, half - 1)
            )

        couple = jnp.where(left, to_next, to_last)
        inv = inverse(inner_diag)
        through = mm(inv, couple)
        schur = inverse(inner_diag - mm(couple, swap(through)))
        own = mm(schur, inner_link)
        other = -mm(through, swap(own))
        levels.append((half, left, swap, out, inv, couple, schur, own, other, outer_link))
        outer_diag = outer_diag - mm(outer_link, out(own))
        outer_link = -mm(outer_link, out(other))
        inner_diag, inner_link = outer_diag, outer_link
        half *= 2

    def ends(x):
        return x[..., :1, :], x[..., SUB - 1 :, :]

    side = lax.broadcasted_iota(jnp.int32, (2, lines), 0) == 0
    unit2 = diagonal_block(jnp.ones((2, lines), jnp.float32))
    signed = jnp.where(side, 0.5, -0.5)

    def both(first, second):
        shape = first.shape[:-2] + (2, lines)
        return jnp.where(side, jnp.broadcast_to(first, shape), jnp.broadcast_to(second, shape))

    def swap2(x):
        return both(x[..., 1:, :], x[..., :1, :])

    def put(buffer, r, pieces, send, recv):
        for i, piece in enumerate(pieces):
            buffer[r, bits[r], i] = piece
        copy = remote(
            buffer.at[r, bits[r]], buffer.at[r, bits[r]], send.at[r], recv.at[r],
            (partners[r], row),
        )
        copy.start()
        return copy

    group = [
        both(*ends(outer_diag)), both(*ends(outer_link)),
        both(jac[:, :, :1, :], jac[:, :, cells - 1 :, :]),
    ]
    mat_copy = put(mats, 0, group, mat_send, mat_recv)

    loads[3].wait()

    @pl.when(has_below)
    def _():
        up_copy.wait_recv()
        down_copy.wait_send()

    @pl.when(has_above)
    def _():
        down_copy.wait_recv()
        up_copy.wait_send()

    tails = jnp.where(has_below, halo_in[0].astype(jnp.float32), 0.0)
    heads = jnp.where(has_above, halo_in[1].astype(jnp.float32), 0.0)
    for f in range(UNK):
        field = flux[f].astype(jnp.float32)
        tail = tails if f == 0 else pltpu.roll(tails, lines - NZ * f, 1)
        head = pltpu.roll(heads, lines - NZ - NZ * f, 1)
        behind = jnp.where(lane < NZ, tail, pltpu.roll(field, NZ, 1))
        ahead = jnp.where(lane >= lines - NZ, head, pltpu.roll(field, lines - NZ, 1))
        res[f] = source[f].astype(jnp.float32) - 0.5 * (ahead - behind)

    rhs = [res[:, pl.ds(t, SUB, stride=STEPS), :] for t in range(STEPS)]
    y1 = mv(schur1, rhs[1] - mv(up12, rhs[2] * over2))
    y2 = mv(schur2, rhs[2] - mv(low21, rhs[1] * over1))
    head_rhs = rhs[0] - mv(up0, y1)
    tail_rhs = rhs[3] - mv(low3, y2)
    inner_rhs = jnp.where(even, tail_rhs, head_rhs)
    outer_rhs = jnp.where(even, head_rhs, tail_rhs)
    ys = []
    for half, left, swap, out, inv, couple, schur, own, other, link in levels:
        y = mv(schur, inner_rhs - mv(couple, swap(mv(inv, inner_rhs))))
        ys.append(y)
        outer_rhs = outer_rhs - mv(link, out(y))
        inner_rhs = outer_rhs
    ends_rhs = both(*ends(outer_rhs))

    merged = []
    for r in range(rounds - 1):
        if r > 0:
            mat_copy = put(mats, r, group, mat_send, mat_recv)
        rhs_copy = put(rhss, r, [ends_rhs], rhs_send, rhs_recv)
        mat_copy.wait()

        def inner(ref, i):
            return both(ref[r, 0, i][..., 1:, :], ref[r, 1, i][..., :1, :])

        def outer(ref, i):
            return jnp.where(side, ref[r, 0, i], ref[r, 1, i])

        couple = swap2(inner(mats, 2)) * signed - damping * unit2
        diag_in, link_in = inner(mats, 0), inner(mats, 1)
        diag_out, link_out = outer(mats, 0), outer(mats, 1)
        inv = inverse(diag_in)
        through = mm(inv, couple)
        schur = inverse(diag_in - mm(couple, swap2(through)))
        own = mm(schur, link_in)
        other = -mm(through, swap2(own))
        group = [
            diag_out - mm(link_out, own), -mm(link_out, other), outer(mats, 2),
        ]
        rhs_copy.wait()
        rhs_in = inner(rhss, 0)
        y = mv(schur, rhs_in - mv(couple, swap2(mv(inv, rhs_in))))
        ends_rhs = outer(rhss, 0) - mv(link_out, y)
        merged.append((own, other, y))

    final = rounds - 1
    is_left = bits[final] == 0
    inv = inverse(group[0])
    far = mm(inv, group[1])
    far_y = mv(inv, ends_rhs)

    def facing(x):
        return jnp.where(is_left, x[..., 1:, :], x[..., :1, :])

    mine = facing(group[0] - mm(group[1], swap2(far)))
    mine_rhs = facing(ends_rhs - mv(group[1], swap2(far_y)))
    mine_jac = facing(group[2])
    last[bits[final], :UNK] = mine
    last[bits[final], UNK : 2 * UNK] = mine_jac
    last[bits[final], 2 * UNK] = mine_rhs
    last_copy = remote(
        last.at[bits[final]], last.at[bits[final]], last_send, last_recv, (partners[final], row)
    )
    last_copy.start()
    last_copy.wait()
    theirs = 1 - bits[final]
    their_jac = last[theirs, UNK : 2 * UNK]
    unit1 = diagonal_block(jnp.ones((1, lines), jnp.float32))
    my_couple = their_jac * jnp.where(is_left, 0.5, -0.5) - damping * unit1
    their_couple = mine_jac * jnp.where(is_left, -0.5, 0.5) - damping * unit1
    inv = inverse(last[theirs, :UNK])
    meeting = solve_one(
        mine - mm(my_couple, mm(inv, their_couple)),
        mine_rhs - mv(my_couple, mv(inv, last[theirs, 2 * UNK])),
    )
    shape2 = (UNK, 2, lines)
    at_far = far_y - mv(far, jnp.broadcast_to(meeting, shape2))
    x_head = jnp.where(is_left, at_far[:, :1], meeting)
    x_tail = jnp.where(is_left, meeting, at_far[:, 1:])
    for r in reversed(range(rounds - 1)):
        own, other, y = merged[r]
        found = y - mv(own, both(x_head, x_tail)) - mv(other, both(x_tail, x_head))
        x_head, x_tail = (
            jnp.where(bits[r] == 0, x_head, found[:, 1:]),
            jnp.where(bits[r] == 0, found[:, :1], x_tail),
        )

    shape = (UNK, SUB, lines)
    current = jnp.where(
        sub < SUB // 2, jnp.broadcast_to(x_head, shape), jnp.broadcast_to(x_tail, shape)
    )
    for (half, left, swap, out, inv, couple, schur, own, other, link), y in zip(
        reversed(levels), reversed(ys)
    ):
        near = current if half == 1 else jnp.where(
            left, sub_roll(current, half - 1), sub_roll(current, 1 - half)
        )
        away = jnp.where(left, sub_roll(current, -half), sub_roll(current, half))
        found = y - mv(own, near) - mv(other, away)
        if half > 1:
            place = lax.rem(sub, 2 * half)
            current = jnp.where((place == half - 1) | (place == half), found, current)
    x0 = jnp.where(even, current, found)
    x3 = jnp.where(even, found, current)
    x1 = y1 - mv(own1, x0) - mv(other1, x3)
    x2 = y2 - mv(own2, x3) - mv(other2, x0)
    for t, value in enumerate((x0, x1, x2, x3)):
        out_ref[:, pl.ds(t, SUB, stride=STEPS), :] = value


def shards(line_size, cross_size, jacobian, time_step, source, cross_flux):
    cells, lines = time_step.shape
    rounds = line_size.bit_length() - 1
    assert line_size == 1 << rounds and rounds >= 2 and cross_size >= 3
    assert cells == SUB * STEPS
    f32, bf16 = jnp.float32, jnp.bfloat16
    dma = pltpu.SemaphoreType.DMA
    return pl.pallas_call(
        functools.partial(kernel, line_size, cross_size),
        out_shape=pltpu.VMEM((UNK, cells, lines), f32),
        in_specs=[pl.BlockSpec(memory_space=pl.ANY)] * 4,
        out_specs=pl.BlockSpec(memory_space=pltpu.VMEM),
        scratch_shapes=[
            pltpu.VMEM((UNK, UNK, cells, lines), f32),
            pltpu.VMEM((cells, lines), f32),
            pltpu.VMEM((UNK, cells, lines), bf16),
            pltpu.VMEM((UNK, cells, lines), bf16),
            pltpu.VMEM((UNK, cells, lines), f32),
            pltpu.VMEM((2, cells, lines), bf16),
            pltpu.VMEM((2, cells, lines), bf16),
            pltpu.VMEM((rounds - 1, 2, 3, UNK, UNK, 2, lines), f32),
            pltpu.VMEM((rounds - 1, 2, 1, UNK, 2, lines), f32),
            pltpu.VMEM((2, 2 * UNK + 1, UNK, 1, lines), f32),
            dma((4,)),
            dma((2,)), dma((2,)),
            dma((rounds - 1,)), dma((rounds - 1,)),
            dma((rounds - 1,)), dma((rounds - 1,)),
            dma, dma,
        ],
        compiler_params=pltpu.CompilerParams(
            collective_id=0, has_side_effects=True, vmem_limit_bytes=VMEM_BYTES
        ),
        name="sweep",
    )(jacobian, time_step, source, cross_flux)


def solution(mesh):
    placed = (
        P(None, None, "line", "cross"),
        P("line", "cross"),
        P(None, "line", "cross"),
        P(None, "line", "cross"),
    )
    return jax.shard_map(
        functools.partial(shards, mesh.shape["line"], mesh.shape["cross"]),
        mesh=mesh, in_specs=placed, out_specs=P(None, "line", "cross"), check_vma=False,
    )
```
